128 devices in a mesh: dp: 8 (over y, core), seq: 16 (over x, z).
Axes of the slice: x: 4, y: 4, z: 4, core: 2. Of those that a mesh axis runs over, the one named last changes fastest.
Arguments:
- tokens: bfloat16 [8, 2048, 768], P('dp', 'seq'), may hold values from -6 to 6
- out_grad: bfloat16 [8, 2048, 768], P('dp', 'seq'), may hold values from -6 to 6
- offsets: int32 [8, 2048], P('dp', 'seq'), may hold values from 0 to 2045, as said below
- ln1_gain: bfloat16 [2, 768], replicated, may hold values from 0.099609375 to 1.8984375
- ln1_bias: bfloat16 [2, 768], replicated, may hold values from -1.75 to 1.75
- in_weight: bfloat16 [2, 768, 2304], replicated, may hold values from -0.21875 to 0.21875
- in_bias: bfloat16 [2, 2304], replicated, may hold values from -1.75 to 1.75
- short_weight: bfloat16 [2, 3, 2304], replicated, may hold values from -3.5 to 3.5
- short_bias: bfloat16 [2, 2304], replicated, may hold values from -1.75 to 1.75
- filter_w1: bfloat16 [2, 33, 64], replicated, may hold values from -1 to 1
- filter_b1: bfloat16 [2, 64], replicated, may hold values from -6 to 6
- filter_w2: bfloat16 [2, 64, 1536], replicated, may hold values from -0.375 to 0.375
- filter_window: float32 [2, 1536], replicated, may hold values from 0.02 to 0.3
- decay_rate: float32 [2, 1536], replicated, may hold values from 4.8828126e-05 to 0.05
- out_weight: bfloat16 [2, 768, 768], replicated, may hold values from -0.21875 to 0.21875
- out_bias: bfloat16 [2, 768], replicated, may hold values from -1.75 to 1.75
- ln2_gain: bfloat16 [2, 768], replicated, may hold values from 0.099609375 to 1.8984375
- ln2_bias: bfloat16 [2, 768], replicated, may hold values from -1.75 to 1.75
- fc1_weight: bfloat16 [2, 768, 3072], replicated, may hold values from -0.21875 to 0.21875
- fc1_bias: bfloat16 [2, 3072], replicated, may hold values from -1.75 to 1.75
- fc2_weight: bfloat16 [2, 3072, 768], replicated, may hold values from -0.109375 to 0.109375
- fc2_bias: bfloat16 [2, 768], replicated, may hold values from -1.75 to 1.75
Outputs:
- mixed: bfloat16 [8, 2048, 768], P('dp', 'seq')
- input_grad: float32 [8, 2048, 768], P('dp', 'seq')
- grad_ln1_gain: float32 [2, 768], P(None, 'dp')
- grad_ln1_bias: float32 [2, 768], P(None, 'dp')
- grad_in_weight: float32 [2, 768, 2304], P(None, 'dp')
- grad_in_bias: float32 [2, 2304], P(None, 'dp')
- grad_short_weight: float32 [2, 3, 2304], P(None, None, 'dp')
- grad_short_bias: float32 [2, 2304], P(None, 'dp')
- grad_filter_w1: float32 [2, 33, 64], P(None, None, 'dp')
- grad_filter_b1: float32 [2, 64], P(None, 'dp')
- grad_filter_w2: float32 [2, 64, 1536], P(None, None, 'dp')
- grad_filter_window: float32 [2, 1536], P(None, 'dp')
- grad_decay_rate: float32 [2, 1536], P(None, 'dp')
- grad_out_weight: float32 [2, 768, 768], P(None, 'dp')
- grad_out_bias: float32 [2, 768], P(None, 'dp')
- grad_ln2_gain: float32 [2, 768], P(None, 'dp')
- grad_ln2_bias: float32 [2, 768], P(None, 'dp')
- grad_fc1_weight: float32 [2, 768, 3072], P(None, 'dp')
- grad_fc1_bias: float32 [2, 3072], P(None, 'dp')
- grad_fc2_weight: float32 [2, 3072, 768], P(None, 'dp')
- grad_fc2_bias: float32 [2, 768], P(None, 'dp')
The draws below stay inside these ranges and needn't reach their ends.
Inputs may be any that keep to these rules, and one draw needn't show every extreme that they name: Each row is a sequence of whole documents: offsets is 0 at a document's first token and grows by one per token; every row starts a document at its first token; in every row one document starts within the first 128 tokens and ends within the last 128 tokens; in some row that document runs from the second token to the second to last.
All inputs are finite; a program needn't handle non-finite values.
Results may differ from the reference program's by a relative error of at most 0.025.
Values may be sent and summed in bfloat16 or wider, within the bound.
No kernel may reach another device: no remote copies, remote signals or barrier semaphores. Data moves between devices by JAX's collectives and lax.ppermute only.
A program may use at most 256 MiB of HBM per device.

```python
import math
import jax
import jax.numpy as jnp
from jax import lax

D = 768
FF = 3072
FH = 64
POS = 33
TAPS = 16
LAYERS = 2
BLOCK = 128
ROWS = 8
ROW_LEN = 2048


def draw_offsets(key, part):
    key = jax.random.fold_in(key, 11)
    key_first, key_last, key_extra, key_row = jax.random.split(key, 4)
    first_start = jax.random.randint(key_first, (ROWS, 1), 1, BLOCK)
    last_start = ROW_LEN - jax.random.randint(key_last, (ROWS, 1), 1, BLOCK)
    chosen = jax.random.randint(key_row, (), 0, ROWS)
    row_ids = jnp.arange(ROWS, dtype=jnp.int32)[:, None]
    first_start = jnp.where(row_ids == chosen, 1, first_start)
    last_start = jnp.where(row_ids == chosen, ROW_LEN - 1, last_start)
    places = jnp.arange(ROW_LEN, dtype=jnp.int32)[None, :]
    extra = jax.random.randint(key_extra, (ROWS, ROW_LEN), 0, 4) == 0
    outside = (places < first_start) | (places > last_start)
    starts = (places == 0) | (places == first_start) | (places == last_start) | extra & outside
    begins = lax.cummax(jnp.where(starts, places, 0), axis=1)
    return (places - begins).astype(jnp.int32)


def levels(stream_key, shape, pieces, low, high):
    factor_of = 1.0
    for axis_at, blocks in pieces:
        heights = jax.random.uniform(jax.random.fold_in(jax.random.fold_in(stream_key, 6), axis_at), (blocks,), jnp.float32, low / len(pieces), high / len(pieces))
        factor_of = factor_of * jnp.repeat(jnp.exp(heights), shape[axis_at] // blocks).reshape((-1,) + (1,) * (len(shape) - 1 - axis_at))
    return factor_of


def scatter_about(stream_key, dims, width, limit, shards=(), kind=jnp.bfloat16):
    factor_of = levels(stream_key, dims, shards, -0.22, 0.18) if shards else 1.0
    values = jax.random.normal(stream_key, dims, jnp.float32) * width * factor_of
    return jnp.minimum(jnp.maximum(values, -limit), limit).astype(kind)


def setup_inputs(seed: int = 0) -> dict:
    key_of = jax.random.split(jax.random.key(seed), 23)
    tokens = scatter_about(key_of[0], (ROWS, ROW_LEN, D), 1.0, 6.0, ((0, 8), (1, 16)))
    out_grad = scatter_about(key_of[1], (ROWS, ROW_LEN, D), 1.0, 6.0, ((0, 8), (1, 16)))
    offsets = draw_offsets(jax.random.fold_in(key_of[22], 71), 0)
    ln1_gain = jnp.clip(1.0 + 0.18 * jax.random.normal(key_of[3], (LAYERS, D), jnp.float32), 0.099609375, 1.8984375).astype(jnp.bfloat16)
    ln1_bias = scatter_about(key_of[4], (LAYERS, D), 0.3, 1.75)
    in_weight = scatter_about(key_of[5], (LAYERS, D, 3 * D), D ** -0.5, 0.21875)
    in_bias = scatter_about(key_of[6], (LAYERS, 3 * D), 0.3, 1.75)
    short_weight = scatter_about(key_of[7], (LAYERS, 3, 3 * D), 0.6, 3.5)
    short_bias = scatter_about(key_of[8], (LAYERS, 3 * D), 0.3, 1.75)
    filter_w1 = scatter_about(key_of[9], (LAYERS, POS, FH), POS ** -0.5, 1.0)
    filter_b1 = scatter_about(key_of[10], (LAYERS, FH), 1.0, 6.0)
    filter_w2 = scatter_about(key_of[11], (LAYERS, FH, 2 * D), (4 * FH) ** -0.5, 0.375)
    filter_window = jnp.clip(jnp.exp(jax.random.uniform(key_of[12], (LAYERS, 2 * D), jnp.float32, math.log(0.02), math.log(0.3))), 0.02, 0.3)
    decay_rate = jnp.clip(jnp.exp(jax.random.uniform(key_of[13], (LAYERS, 2 * D), jnp.float32, math.log(4.882812572759576e-05), math.log(0.05))), 4.882812572759576e-05, 0.05)
    out_weight = scatter_about(key_of[14], (LAYERS, D, D), D ** -0.5, 0.21875)
    out_bias = scatter_about(key_of[15], (LAYERS, D), 0.3, 1.75)
    ln2_gain = jnp.clip(1.0 + 0.18 * jax.random.normal(key_of[16], (LAYERS, D), jnp.float32), 0.099609375, 1.8984375).astype(jnp.bfloat16)
    ln2_bias = scatter_about(key_of[17], (LAYERS, D), 0.3, 1.75)
    fc1_weight = scatter_about(key_of[18], (LAYERS, D, FF), D ** -0.5, 0.21875)
    fc1_bias = scatter_about(key_of[19], (LAYERS, FF), 0.3, 1.75)
    fc2_weight = scatter_about(key_of[20], (LAYERS, FF, D), FF ** -0.5, 0.109375)
    fc2_bias = scatter_about(key_of[21], (LAYERS, D), 0.3, 1.75)
    return {"tokens": tokens, "out_grad": out_grad, "offsets": offsets, "ln1_gain": ln1_gain, "ln1_bias": ln1_bias, "in_weight": in_weight, "in_bias": in_bias, "short_weight": short_weight, "short_bias": short_bias, "filter_w1": filter_w1, "filter_b1": filter_b1, "filter_w2": filter_w2, "filter_window": filter_window, "decay_rate": decay_rate, "out_weight": out_weight, "out_bias": out_bias, "ln2_gain": ln2_gain, "ln2_bias": ln2_bias, "fc1_weight": fc1_weight, "fc1_bias": fc1_bias, "fc2_weight": fc2_weight, "fc2_bias": fc2_bias}


@jax.custom_vjp
def low(v):
    return lax.optimization_barrier(v.astype(jnp.bfloat16)).astype(jnp.float32)

@jax.custom_vjp
def low_back(v):
    return v

def low_keep(v):
    return (low(v), None)

def low_pass(kept, grad):
    return (grad,)

def back_keep(v):
    return (v, None)

def back_low(kept, grad):
    return (low(grad),)
low.defvjp(low_keep, low_pass)
low_back.defvjp(back_keep, back_low)
highest = lax.Precision.HIGHEST

def layer_norm(stream, gain, offset_bias):
    average = lax.optimization_barrier(jnp.mean(stream, axis=-1, keepdims=True))
    centered = stream - average
    variance = lax.optimization_barrier(jnp.mean(centered * centered, axis=-1, keepdims=True))
    return centered * lax.rsqrt(variance + 1e-05) * gain + offset_bias

def positions(place_count, feature_count):
    band_count = (feature_count - 1) // 2
    places = jnp.arange(place_count, dtype=jnp.float32)[:, None]
    angles = jnp.arange(1, band_count + 1, dtype=jnp.float32)[None, :] * (math.pi / (band_count + 1))
    return jnp.concatenate([places / place_count, jnp.cos(places * angles), jnp.sin(places * angles)], axis=1)

def make_filter(weight_one, bias_one, weight_two, window, decay_rate, tap_count):
    features = positions(tap_count + 1, weight_one.shape[0])
    hidden = jnp.sin(jnp.dot(features, weight_one, precision=highest, preferred_element_type=jnp.float32) + bias_one)
    filter_raw = jnp.dot(hidden, weight_two, precision=highest, preferred_element_type=jnp.float32)
    distances = jnp.arange(tap_count + 1, dtype=jnp.float32)[:, None]
    shaped = filter_raw * jnp.exp(-window * distances)
    retain = jnp.exp(-decay_rate)
    tail_gain = shaped[tap_count] * jnp.sqrt(-jnp.expm1(-2.0 * decay_rate))
    return (shaped[:tap_count], tail_gain, retain)

def join_pair(earlier, later):
    return (earlier[0] * later[0], later[0] * earlier[1] + later[1])

def prefix_scan(values, offs, retain):
    factor = jnp.where(offs[..., None] > 0, retain, 0.0)
    return lax.associative_scan(join_pair, (factor, values), axis=1)

def tap_mix(values, halo, offs, tap_values):
    tap_count = tap_values.shape[0]
    length = values.shape[1]
    extended = jnp.concatenate([halo, values], axis=1)
    summed = jnp.zeros_like(values)
    for distance in range(tap_count):
        shifted = extended[:, tap_count - 1 - distance:tap_count - 1 - distance + length]
        summed = summed + jnp.where(offs[..., None] >= distance, shifted, 0.0) * tap_values[distance]
    return summed

def tail_mix(factor, running, carry, offs, tail_gain):
    states = running + factor * carry[:, None, :]
    before = jnp.concatenate([carry[:, None, :], states[:, :-1]], axis=1)
    return jnp.where(offs[..., None] > 0, before, 0.0) * tail_gain

def long_mix(values, halo, carry, offs, tap_values, tail_gain, retain):
    factor, running = prefix_scan(values, offs, retain)
    return tap_mix(values, halo, offs, tap_values) + tail_mix(factor, running, carry, offs, tail_gain)

def project(inputs, weight):
    return jnp.einsum('rtd,df->rtf', inputs, weight, precision=highest, preferred_element_type=jnp.float32)

def apply_layer(stream, offs, params):
    gain_one, bias_one, in_weight, in_bias, short_weight, short_bias, filter_w1, filter_b1, filter_w2, filter_window, decay_rate, out_weight, out_bias, gain_two, bias_two, fc1_weight, fc1_bias, fc2_weight, fc2_bias = params
    model_width = stream.shape[-1]
    row_count = stream.shape[0]
    normed = low(layer_norm(stream, gain_one, bias_one))
    projected = low(low_back(project(normed, in_weight)) + in_bias)
    short_halo = jnp.zeros((row_count, short_weight.shape[0] - 1, projected.shape[-1]), jnp.float32)
    short = tap_mix(projected, short_halo, offs, short_weight) + short_bias
    gate_one = short[..., :model_width]
    gate_two = short[..., model_width:2 * model_width]
    values = low(short[..., 2 * model_width:])
    tap_values, tail_gain, retain = make_filter(filter_w1, filter_b1, filter_w2, filter_window, decay_rate, TAPS)
    long_halo = jnp.zeros((row_count, TAPS - 1, model_width), jnp.float32)
    carry = jnp.zeros((row_count, model_width), jnp.float32)
    inner = low(gate_one * long_mix(values, long_halo, carry, offs, tap_values[:, :model_width], tail_gain[:model_width], retain[:model_width]))
    outer = low(gate_two * long_mix(inner, long_halo, carry, offs, tap_values[:, model_width:], tail_gain[model_width:], retain[model_width:]))
    middle = stream + low_back(project(outer, out_weight)) + out_bias
    normed_two = low(layer_norm(middle, gain_two, bias_two))
    hidden = low(jax.nn.gelu(low_back(project(normed_two, fc1_weight)) + fc1_bias))
    return middle + low_back(project(hidden, fc2_weight)) + fc2_bias

def reference(tokens, out_grad, offsets, ln1_gain, ln1_bias, in_weight, in_bias, short_weight, short_bias, filter_w1, filter_b1, filter_w2, filter_window, decay_rate, out_weight, out_bias, ln2_gain, ln2_bias, fc1_weight, fc1_bias, fc2_weight, fc2_bias):
    weights = tuple((member.astype(jnp.float32) for member in (ln1_gain, ln1_bias, in_weight, in_bias, short_weight, short_bias, filter_w1, filter_b1, filter_w2, filter_window, decay_rate, out_weight, out_bias, ln2_gain, ln2_bias, fc1_weight, fc1_bias, fc2_weight, fc2_bias)))

    def one_row(totals, element):
        row_tokens, row_grad, row_offsets = element
        offs = row_offsets[None]

        def forward(params, stream):
            for layer_index in range(LAYERS):
                stream = apply_layer(stream, offs, tuple((member[layer_index] for member in params)))
            return stream
        result, pullback = jax.vjp(forward, weights, row_tokens[None].astype(jnp.float32))
        weight_grads, input_grad = pullback(row_grad[None].astype(jnp.float32))
        totals = jax.tree.map(jnp.add, totals, weight_grads)
        return (totals, (result[0].astype(jnp.bfloat16), input_grad[0]))
    zero_grads = jax.tree.map(jnp.zeros_like, weights)
    totals, (outputs, input_grads) = lax.scan(one_row, zero_grads, (tokens, out_grad, offsets))
    return (outputs, input_grads, totals[0], totals[1], totals[2], totals[3], totals[4], totals[5], totals[6], totals[7], totals[8], totals[9], totals[10], totals[11], totals[12], totals[13], totals[14], totals[15], totals[16], totals[17], totals[18])
```

```python
import functools
import math
import typing

import jax
import jax.numpy as jnp
import numpy as np
from jax import lax
from jax.experimental import pallas as pl
from jax.experimental.pallas import tpu as pltpu
from jax.sharding import PartitionSpec as P

SEQ = "seq"
DP = "dp"
TAPS = 16
LAYERS = 2
D = 768
FF = 3072
BLK = 128
LANES = 128
TILES = D // LANES
F32 = jnp.float32
BF16 = jnp.bfloat16
highest = lax.Precision.HIGHEST

LENGTHS = (192, 160)

VMEM_LIMIT = 14 * 1024 * 1024


def in_hbm(value):
    return pltpu.with_memory_space_constraint(value, pltpu.HBM)


def vmem():
    return pl.BlockSpec(memory_space=pltpu.VMEM)


def smem():
    return pl.BlockSpec(memory_space=pltpu.SMEM)


NEAR, SCALARS, FAR = range(3)


def run(kernel, ins, outs, scratch=(), limit=VMEM_LIMIT):
    ins = [(item + (None,))[:3] for item in ins]
    outs = [(item + (NEAR,))[:3] for item in outs]
    far_ins = [i for i, item in enumerate(ins) if item[0] == FAR]
    far_outs = [i for i, item in enumerate(outs) if item[2] == FAR]

    def part(item):
        if item[2] is None:
            return item[1].shape
        return jax.eval_shape(lambda x: x[item[2]], item[1]).shape

    buffers = [pltpu.VMEM(part(ins[i]), ins[i][1].dtype) for i in far_ins]
    buffers += [pltpu.VMEM(outs[i][0], outs[i][1]) for i in far_outs]

    def whole(*refs):
        in_refs = list(refs[: len(ins)])
        out_refs = list(refs[len(ins) : len(ins) + len(outs)])
        rest = refs[len(ins) + len(outs) :]
        stores = rest[: len(buffers)]
        sems = rest[-1]
        copies = []
        for n, i in enumerate(far_ins):
            index = ins[i][2]
            if isinstance(index, slice):
                index = pl.ds(index.start, index.stop - index.start)
            source = in_refs[i] if index is None else in_refs[i].at[index]
            copies.append(pltpu.make_async_copy(source, stores[n], sems.at[n]))
            in_refs[i] = stores[n]
        for copy in copies:
            copy.start()
        copies_out = []
        for n, i in enumerate(far_outs, len(far_ins)):
            copies_out.append(pltpu.make_async_copy(stores[n], out_refs[i], sems.at[n]))
            out_refs[i] = stores[n]
        for copy in copies:
            copy.wait()
        kernel(*in_refs, *out_refs, *rest[len(buffers) : -1])
        for copy in copies_out:
            copy.start()
        for copy in copies_out:
            copy.wait()

    spaces = {NEAR: pltpu.VMEM, SCALARS: pltpu.SMEM, FAR: pltpu.HBM}
    return pl.pallas_call(
        whole,
        out_shape=[
            pltpu.HBM(shape, dtype) if kind == FAR else jax.ShapeDtypeStruct(shape, dtype)
            for shape, dtype, kind in outs
        ],
        in_specs=[pl.BlockSpec(memory_space=spaces[item[0]]) for item in ins],
        out_specs=[pl.BlockSpec(memory_space=spaces[item[2]]) for item in outs],
        scratch_shapes=buffers
        + [pltpu.VMEM(shape, dtype) for shape, dtype in scratch]
        + [pltpu.SemaphoreType.DMA((max(1, len(buffers)),))],
        compiler_params=pltpu.CompilerParams(vmem_limit_bytes=limit),
    )(*(in_hbm(x) if kind == FAR else x for kind, x, _ in ins))


def rows_iota(start, count):
    return lax.broadcasted_iota(jnp.int32, (count, LANES), 0) + start


def chunks(start, stop):
    half = (stop - start) // 16 * 8
    return ((start, start + half), (start + half, stop))


def keep(mask, value):
    return jnp.where(mask, value, 0.0)


def powers(rate, exponent):
    return jnp.exp(-rate * exponent.astype(F32))


def scan_forward(src, offs, dst, rate, start, stop, base_src, base_dst):
    lane = lax.broadcasted_iota(jnp.int32, (8, LANES), 0)
    r1 = jnp.exp(-rate)
    r2 = r1 * r1
    r4 = r2 * r2
    climb = powers(rate, lane + 1)
    carry = None
    for row in range(start, stop, 8):
        o = offs[row : row + 8, :]
        reach = jnp.minimum(o, lane)
        y = src[base_src + row : base_src + row + 8, :]
        y = y + keep(reach >= 1, pltpu.roll(y, 1, 0) * r1)
        y = y + keep(reach >= 2, pltpu.roll(y, 2, 0) * r2)
        y = y + keep(reach >= 4, pltpu.roll(y, 4, 0) * r4)
        if carry is not None:
            y = y + keep(o >= lane + 1, climb * carry)
        dst[base_dst + row : base_dst + row + 8, :] = y
        carry = jnp.broadcast_to(y[7:8, :], (8, LANES))


def scan_backward(src, offs, dst, rate, start, stop, base_src, base_dst):
    lane = lax.broadcasted_iota(jnp.int32, (8, LANES), 0)
    r1 = jnp.exp(-rate)
    r2 = r1 * r1
    r4 = r2 * r2
    climb = powers(rate, 8 - lane)
    carry = None
    ahead = None
    for row in range(stop - 8, start - 1, -8):
        o = offs[row : row + 8, :]
        reach = jnp.minimum(o, lane)
        y = src[base_src + row : base_src + row + 8, :]
        y = y + pltpu.roll(keep(reach >= 1, y * r1), 7, 0)
        y = y + pltpu.roll(keep(reach >= 2, y * r2), 6, 0)
        y = y + pltpu.roll(keep(reach >= 4, y * r4), 4, 0)
        if carry is not None:
            y = y + keep(ahead >= 8 - lane, climb * carry)
        dst[base_dst + row : base_dst + row + 8, :] = keep(o > 0, y)
        carry = jnp.broadcast_to(y[0:1, :], (8, LANES))
        ahead = jnp.broadcast_to(o[0:1, :], (8, LANES))


def front_kernel(
    length, proj, offs, sw, fp, gate1, gate2, vals, yloc, sloc, summ, ps, vs, ss
):
    last = length - 1
    zeros16 = jnp.zeros((16, LANES), F32)

    def tile(c, carry):
        col = pl.multiple_of(c * LANES, LANES)
        one = pl.ds(col, LANES)
        two = pl.ds(pl.multiple_of(col + D, LANES), LANES)
        ps[0:16, :] = zeros16
        vs[0:16, :] = zeros16
        ss[0:16, :] = zeros16
        ss[8:24, :] = zeros16

        def short(part):
            cols = pl.ds(pl.multiple_of(col + part * D, LANES), LANES)
            ps[16 : 16 + length, :] = proj[:, cols].astype(F32)
            w0, w1, w2, bias = (sw[i : i + 1, cols] for i in range(4))
            out = []
            for lo, hi in chunks(0, length):
                o = offs[lo:hi, :]
                out.append(
                    bias
                    + w0 * ps[16 + lo : 16 + hi, :]
                    + w1 * keep(o >= 1, ps[15 + lo : 15 + hi, :])
                    + w2 * keep(o >= 2, ps[14 + lo : 14 + hi, :])
                )
            return jnp.concatenate(out, axis=0)

        gate1[:, one] = short(0)
        gate2[:, one] = short(1)
        value = short(2).astype(BF16)
        vals[:, one] = value
        vs[16 : 16 + length, :] = value.astype(F32)
        rate1 = fp[17:18, one]
        rate2 = fp[17:18, two]
        tail1 = fp[16:17, one]
        scan_forward(vs, offs, ss, rate1, 16, length, 16, 8)
        sloc[:, one] = ss[8 : 8 + length, :]
        total_a = jnp.zeros((8, LANES), F32)
        total_b = jnp.zeros((8, LANES), F32)
        near = jnp.broadcast_to(offs[last : last + 1, :], (8, LANES))
        for lo, hi in chunks(16, length):
            o = offs[lo:hi, :]
            acc = keep(o > 0, ss[7 + lo : 7 + hi, :]) * tail1
            for k in range(TAPS):
                v = vs[16 + lo - k : 16 + hi - k, :]
                acc = acc + keep(o >= k, v) * fp[k : k + 1, one]
            yloc[lo:hi, one] = acc
        for lo in range(32, 160, 8):
            e = rows_iota(lo, 8)
            o = offs[lo : lo + 8, :]
            weight = keep(near >= last - e, powers(rate2, 159 - e)) * gate1[lo : lo + 8, one]
            total_a = total_a + weight * yloc[lo : lo + 8, one]
            total_b = total_b + weight * keep(o >= e - 15, powers(rate1, e - 16))
        end1 = keep(near[0:1, :] >= last - 143, ss[8 + 143 : 8 + 144, :])
        summ[0:1, one] = end1
        summ[1:2, one] = jnp.sum(total_a, axis=0, keepdims=True)
        summ[2:3, one] = jnp.sum(total_b, axis=0, keepdims=True) * tail1
        summ[3:8, one] = jnp.zeros((5, LANES), F32)
        return carry

    lax.fori_loop(0, TILES, tile, 0)


def pick(values, index):
    out = values[0]
    for i in range(1, len(values)):
        out = jnp.where(index == i, values[i], out)
    return out


def join_kernel(where, own, r1, r2, r3, rates, total, before, pieces):
    z = where[1]
    parts = (own[...], r1[...], r2[...], r3[...])
    rate1, rate2 = rates[0:1, :], rates[1:2, :]
    f1 = jnp.exp(-rate1 * float(BLK))
    f2 = jnp.exp(-rate2 * float(BLK))
    e = jnp.zeros((1, D), F32)
    a = jnp.zeros((1, D), F32)
    b = jnp.zeros((1, D), F32)
    be, ba, bb = e, a, b
    reach = jnp.ones((1, D), F32)
    for i in range(4):
        here = pick(parts, (z - i) & 3)
        be = jnp.where(z == i, e, be)
        ba = jnp.where(z == i, a, ba)
        bb = jnp.where(z == i, b, bb)
        pieces[i : i + 1, :] = here[2:3, :]
        a = f2 * a + here[2:3, :] * e + here[1:2, :]
        b = f2 * b + here[2:3, :] * reach
        e = f1 * e + here[0:1, :]
        reach = reach * f1
    pad = jnp.zeros((5, D), F32)
    total[...] = jnp.concatenate([e, a, b, pad], axis=0)
    before[...] = jnp.concatenate([be, ba, bb, pad], axis=0)
    pieces[4:8, :] = jnp.zeros((4, D), F32)


def join_back_kernel(where, own, r1, r2, r3, pieces, rates, total, after):
    z = where[1]
    parts = (own[...], r1[...], r2[...], r3[...])
    rate1, rate2 = rates[0:1, :], rates[1:2, :]
    f1 = jnp.exp(-rate1 * float(BLK))
    f2 = jnp.exp(-rate2 * float(BLK))
    c1 = jnp.zeros((1, D), F32)
    c2 = jnp.zeros((1, D), F32)
    b = jnp.zeros((1, D), F32)
    s1, s2, sb = c1, c2, b
    reach = jnp.ones((1, D), F32)
    for i in (3, 2, 1, 0):
        here = pick(parts, (z - i) & 3)
        s1 = jnp.where(z == i, c1, s1)
        s2 = jnp.where(z == i, c2, s2)
        sb = jnp.where(z == i, b, sb)
        through = pieces[i : i + 1, :]
        c1 = f1 * c1 + through * c2 + here[0:1, :]
        c2 = f2 * c2 + here[1:2, :]
        b = f1 * b + through * reach
        reach = reach * f2
    total[...] = jnp.concatenate([c1, c2, jnp.zeros((6, D), F32)], axis=0)
    after[...] = jnp.concatenate([s1, s2, sb, jnp.zeros((5, D), F32)], axis=0)


def rest_kernel(
    length,
    where,
    before,
    g1,
    g2,
    g3,
    gate1,
    gate2,
    yloc,
    offs,
    fp,
    inner,
    outer,
    conv2,
    state2,
    carry,
    through,
    ins,
    ss,
):
    x = where[0]
    z = where[1].astype(F32)
    for i, far in enumerate((g1, g2, g3)):
        through[i : i + 1, :] = far[2:3, :]
    through[3:8, :] = jnp.zeros((5, D), F32)
    zeros16 = jnp.zeros((16, LANES), F32)

    def tile(c, unused):
        col = pl.multiple_of(c * LANES, LANES)
        one = pl.ds(col, LANES)
        two = pl.ds(pl.multiple_of(col + D, LANES), LANES)
        rate1 = fp[17:18, one]
        rate2 = fp[17:18, two]
        tail1 = fp[16:17, one]
        tail2 = fp[16:17, two]
        f1 = jnp.exp(-rate1 * float(4 * BLK))
        f2 = jnp.exp(-rate2 * float(4 * BLK))
        parts = (g1[:, one], g1[:, one], g2[:, one], g3[:, one])
        c1 = jnp.zeros((1, LANES), F32)
        c2 = jnp.zeros((1, LANES), F32)
        for i in range(3):
            here = pick(parts, (x - i) & 3)
            n2 = f2 * c2 + here[1:2, :] + here[2:3, :] * c1
            n1 = f1 * c1 + here[0:1, :]
            c1 = jnp.where(i < x, n1, c1)
            c2 = jnp.where(i < x, n2, c2)
        c2 = jnp.exp(-rate2 * BLK * z) * c2 + before[1:2, one] + before[2:3, one] * c1
        c1 = jnp.exp(-rate1 * BLK * z) * c1 + before[0:1, one]
        carry[0:1, one] = c1
        carry[1:2, one] = c2
        carry[2:8, one] = jnp.zeros((6, LANES), F32)
        ins[0:16, :] = zeros16
        for lo in range(16, length, 16):
            e = rows_iota(lo, 16)
            o = offs[lo : lo + 16, :]
            y = yloc[lo : lo + 16, one] + keep(o >= e - 15, powers(rate1, e - 16)) * (tail1 * c1)
            low = (gate1[lo : lo + 16, one] * y).astype(BF16)
            inner[lo : lo + 16, one] = low
            ins[lo : lo + 16, :] = low.astype(F32)
        inner[0:16, one] = zeros16.astype(BF16)
        ss[0:40, :] = jnp.zeros((40, LANES), F32)
        scan_forward(ins, offs, ss, rate2, 32, length, 0, 8)
        for lo, hi in chunks(32, length):
            o = offs[lo:hi, :]
            e = rows_iota(lo, hi - lo)
            s = keep(o > 0, ss[7 + lo : 7 + hi, :])
            s = s + keep(o >= e - 31, powers(rate2, e - 32)) * c2
            state2[lo - 32 : hi - 32, one] = s
            acc = s * tail2
            for k in range(TAPS):
                acc = acc + keep(o >= k, ins[lo - k : hi - k, :]) * fp[k : k + 1, two]
            conv2[lo - 32 : hi - 32, one] = acc
        outer[:, one] = (gate2[32:length, one] * conv2[:, one]).astype(BF16)
        return unused

    lax.fori_loop(0, TILES, tile, 0)


def back_kernel(
    length,
    dout,
    gate1,
    gate2,
    state2,
    inner,
    offs,
    fp,
    dinner,
    sums,
    direct,
    xs,
    dys,
    qs,
    ins,
):
    last = length - 1
    zeros16 = jnp.zeros((16, LANES), F32)

    def tile(c, unused):
        col = pl.multiple_of(c * LANES, LANES)
        one = pl.ds(col, LANES)
        two = pl.ds(pl.multiple_of(col + D, LANES), LANES)
        rate1 = fp[17:18, one]
        rate2 = fp[17:18, two]
        tail1 = fp[16:17, one]
        tail2 = fp[16:17, two]
        dys[0:16, :] = zeros16
        dys[16:32, :] = zeros16
        dys[length : length + 16, :] = zeros16
        dy = dout[:, one] * gate2[32:length, one]
        dys[32:length, :] = dy
        xs[32:length, :] = dy * tail2
        qs[0:16, :] = zeros16
        qs[16:32, :] = zeros16
        qs[length : length + 8, :] = jnp.zeros((8, LANES), F32)
        scan_backward(xs, offs, qs, rate2, 32, length, 0, 0)
        direct[1:2, one] = qs[32:33, :]
        ins[...] = inner[:, one].astype(F32)
        near = offs[last : last + 1, :]
        tap_sums = [jnp.zeros((8, LANES), F32) for _ in range(TAPS)]
        d1 = jnp.zeros((8, LANES), F32)

        def fold(value):
            out = value[0:8]
            for i in range(8, value.shape[0], 8):
                out = out + value[i : i + 8]
            return out

        for lo, hi in chunks(16, length):
            acc = jnp.zeros((hi - lo, LANES), F32)
            v = ins[lo:hi, :]
            for k in range(TAPS):
                m = keep(offs[lo + k : hi + k, :] >= k, dys[lo + k : hi + k, :])
                acc = acc + m * fp[k : k + 1, two]
                tap_sums[k] = tap_sums[k] + fold(m * v)
            e = rows_iota(lo, hi - lo)
            acc = acc + keep(e >= 32, qs[lo + 1 : hi + 1, :])
            dinner[lo:hi, one] = acc
            o = offs[lo:hi, :]
            reach = keep(o >= e - 15, powers(rate1, e - 16))
            d1 = d1 + fold(reach * gate1[lo:hi, one] * acc)
        dinner[0:16, one] = zeros16
        direct[0:1, one] = jnp.sum(d1, axis=0, keepdims=True) * tail1
        direct[2:8, one] = jnp.zeros((6, LANES), F32)
        for k in range(TAPS):
            sums[k : k + 1, one] = jnp.sum(tap_sums[k], axis=0, keepdims=True)
        t_tail = jnp.zeros((8, LANES), F32)
        t_own = jnp.zeros((8, LANES), F32)
        t_next = jnp.zeros((8, LANES), F32)
        for lo in range(32, length, 8):
            s = state2[lo - 32 : lo - 24, one]
            t_tail = t_tail + s * dys[lo : lo + 8, :]
            t_own = t_own + s * qs[lo + 1 : lo + 9, :]
            if lo < 160:
                e = rows_iota(lo, 8)
                t_next = t_next + s * keep(near >= last - e, powers(rate2, 159 - e))
        sums[16:17, one] = jnp.sum(t_tail, axis=0, keepdims=True)
        sums[17:18, one] = jnp.sum(t_own, axis=0, keepdims=True)
        sums[18:19, one] = jnp.sum(t_next, axis=0, keepdims=True)
        sums[19:24, one] = jnp.zeros((5, LANES), F32)
        return unused

    lax.fori_loop(0, TILES, tile, 0)


def end_kernel(
    length,
    where,
    after,
    h1,
    h2,
    h3,
    through_of,
    dinner,
    dout,
    conv2,
    gate1,
    yloc,
    sloc,
    vals,
    carry,
    proj,
    offs,
    sw,
    fp,
    sums,
    dproj,
    colsums,
    filt,
    xs,
    dys,
    qs,
    ds,
    ss,
):
    last = length - 1
    x = where[0]
    later = (3 - where[1]).astype(F32)
    zeros16 = jnp.zeros((16, LANES), F32)

    def fold(value):
        out = value[0:8]
        for i in range(8, value.shape[0], 8):
            out = out + value[i : i + 8]
        return out

    def total(value):
        return jnp.sum(value, axis=0, keepdims=True)

    def tile(c, unused):
        col = pl.multiple_of(c * LANES, LANES)
        one = pl.ds(col, LANES)
        two = pl.ds(pl.multiple_of(col + D, LANES), LANES)
        three = pl.ds(pl.multiple_of(col + 2 * D, LANES), LANES)
        rate1 = fp[17:18, one]
        rate2 = fp[17:18, two]
        tail1 = fp[16:17, one]
        f1 = jnp.exp(-rate1 * float(4 * BLK))
        f2 = jnp.exp(-rate2 * float(4 * BLK))
        steps = (h1[:, one], h1[:, one], h2[:, one], h3[:, one])
        throughs = [through_of[i : i + 1, one] for i in (0, 0, 1, 2)]
        c1 = jnp.zeros((1, LANES), F32)
        c2 = jnp.zeros((1, LANES), F32)
        for i in (3, 2, 1):
            here = pick(steps, (x - i) & 3)
            through = pick(throughs, (x - i) & 3)
            n1 = f1 * c1 + through * c2 + here[0:1, :]
            n2 = f2 * c2 + here[1:2, :]
            c1 = jnp.where(i > x, n1, c1)
            c2 = jnp.where(i > x, n2, c2)
        c1 = jnp.exp(-rate1 * BLK * later) * c1 + after[0:1, one] + after[2:3, one] * c2
        c2 = jnp.exp(-rate2 * BLK * later) * c2 + after[1:2, one]
        near = offs[last : last + 1, :]
        carry1 = carry[0:1, one]

        for lo in (0, 16):
            dys[lo : lo + 16, :] = zeros16
            qs[lo : lo + 16, :] = zeros16
        dys[length : length + 16, :] = zeros16
        qs[length : length + 8, :] = jnp.zeros((8, LANES), F32)
        ds[0:16, :] = zeros16
        ds[length : length + 16, :] = zeros16
        ss[0:16, :] = zeros16
        ss[8 : 8 + length, :] = sloc[:, one]
        ss[8:24, :] = zeros16

        for lo in range(16, length, 8):
            e = rows_iota(lo, 8)
            o = offs[lo : lo + 8, :]
            d = dinner[lo : lo + 8, one]
            if 32 <= lo < 160:
                d = d + keep(near >= last - e, powers(rate2, 159 - e)) * c2
            conv1 = yloc[lo : lo + 8, one] + keep(o >= e - 15, powers(rate1, e - 16)) * (
                tail1 * carry1
            )
            ds[lo : lo + 8, :] = d * conv1
            dy = d * gate1[lo : lo + 8, one]
            dys[lo : lo + 8, :] = dy
            xs[lo : lo + 8, :] = dy * tail1

        def short_back(part, cols):
            w0, w1, w2 = (sw[i : i + 1, cols] for i in range(3))
            sums_of = [jnp.zeros((8, LANES), F32) for _ in range(5)]
            for lo in range(0, length, 16):
                hi = lo + 16
                p = proj[lo:hi, cols].astype(F32)
                m0 = ds[lo:hi, :]
                m1 = keep(offs[lo + 1 : hi + 1, :] >= 1, ds[lo + 1 : hi + 1, :])
                m2 = keep(offs[lo + 2 : hi + 2, :] >= 2, ds[lo + 2 : hi + 2, :])
                out = w0 * m0 + w1 * m1 + w2 * m2
                dproj[lo:hi, cols] = out.astype(BF16)
                for i, value in enumerate((out, p * m0, p * m1, p * m2, m0)):
                    sums_of[i] = sums_of[i] + fold(value)
            for i in range(5):
                colsums[i : i + 1, cols] = total(sums_of[i])
            colsums[5:8, cols] = jnp.zeros((3, LANES), F32)

        short_back(0, one)
        ds[16:32, :] = zeros16
        ds[32:length, :] = dout[:, one] * conv2[:, one]
        short_back(1, two)

        scan_backward(xs, offs, qs, rate1, 16, length, 0, 0)
        tap_sums = [jnp.zeros((8, LANES), F32) for _ in range(TAPS)]
        for lo, hi in chunks(0, length):
            v = vals[lo:hi, one].astype(F32)
            acc = jnp.zeros((hi - lo, LANES), F32)
            for k in range(TAPS):
                m = keep(offs[lo + k : hi + k, :] >= k, dys[lo + k : hi + k, :])
                acc = acc + m * fp[k : k + 1, one]
                tap_sums[k] = tap_sums[k] + fold(m * v)
            ds[lo:hi, :] = acc
        for k in range(TAPS):
            filt[k : k + 1, one] = total(tap_sums[k])
        t_tail = jnp.zeros((8, LANES), F32)
        t_retain = jnp.zeros((8, LANES), F32)
        for lo in range(16, length, 8):
            e = rows_iota(lo, 8)
            o = offs[lo : lo + 8, :]
            g = qs[lo + 1 : lo + 9, :]
            if lo < 144:
                g = g + keep(near >= last - e, powers(rate1, 143 - e)) * c1
            s = keep(o > 0, ss[lo + 7 : lo + 15, :]) + keep(
                o >= e - 15, powers(rate1, e - 16)
            ) * carry1
            t_tail = t_tail + s * dys[lo : lo + 8, :]
            t_retain = t_retain + s * g
            ds[lo : lo + 8, :] = ds[lo : lo + 8, :] + g
        filt[16:17, one] = total(t_tail)
        filt[17:18, one] = total(t_retain)
        filt[18:24, one] = jnp.zeros((6, LANES), F32)
        filt[0:17, two] = sums[0:17, one]
        filt[17:18, two] = sums[17:18, one] + sums[18:19, one] * c2
        filt[18:24, two] = jnp.zeros((6, LANES), F32)
        short_back(2, three)
        return unused

    lax.fori_loop(0, TILES, tile, 0)


def seq_shift(block, along_z, distance):
    pairs = []
    for x in range(4):
        for z in range(4):
            if along_z:
                target = x * 4 + (z + distance) % 4
            else:
                target = (x + distance) % 4 * 4 + z
            pairs.append((x * 4 + z, target))
    return lax.ppermute(block, SEQ, pairs)


def swap(block, axis, bits):
    count = 16 if axis == SEQ else 8
    return lax.ppermute(block, axis, [(i, i ^ bits) for i in range(count)])


def part_shift(block, distance):
    pairs = [(2 * y + c, (y + distance) % 4 * 2 + c) for y in range(4) for c in range(2)]
    return lax.ppermute(block, DP, pairs)


def from_left(block):
    return lax.ppermute(block, SEQ, [(i, i + 1) for i in range(15)])


def from_right(block):
    return lax.ppermute(block, SEQ, [(i + 1, i) for i in range(15)])


def layer_norm(stream, gain, bias):
    average = jnp.mean(stream, axis=-1, keepdims=True)
    centered = stream - average
    variance = jnp.mean(centered * centered, axis=-1, keepdims=True)
    return centered * lax.rsqrt(variance + 1e-05) * gain + bias


def layer_norm_back(stream, gain, grad):
    average = jnp.mean(stream, axis=-1, keepdims=True)
    centered = stream - average
    variance = jnp.mean(centered * centered, axis=-1, keepdims=True)
    scale = lax.rsqrt(variance + 1e-05)
    hat = centered * scale
    grad_gain = jnp.sum(grad * hat, axis=0)
    grad_bias = jnp.sum(grad, axis=0)
    g = grad * gain
    out = scale * (
        g
        - jnp.mean(g, axis=-1, keepdims=True)
        - hat * jnp.mean(g * hat, axis=-1, keepdims=True)
    )
    return out, grad_gain, grad_bias


def positions(place_count, feature_count):
    band_count = (feature_count - 1) // 2
    places = np.arange(place_count, dtype=np.float32)[:, None]
    angles = np.arange(1, band_count + 1, dtype=np.float32)[None, :] * np.float32(
        math.pi / (band_count + 1)
    )
    return np.concatenate(
        [places / np.float32(place_count), np.cos(places * angles), np.sin(places * angles)], axis=1
    )


def dot(a, b):
    return jnp.dot(a, b, preferred_element_type=F32)


def dot_t(a, b):
    return lax.dot_general(a, b, (((1,), (1,)), ((), ())), preferred_element_type=F32)


def dot_w(a, b):
    return lax.dot_general(a, b, (((0,), (0,)), ((), ())), preferred_element_type=F32)


def prepare_kernel(*refs):
    (features, losses, offsets, w1, b1, w2, window, rate, short_weight, short_bias, *vectors) = refs[:18]
    (fp, sw, table, rates, slope, turned, offs, *outs) = refs[18:]
    w1_rows = [w1[j].astype(F32) for j in range(33)]
    short_rows = [short_weight[k].astype(F32) for k in range(3)]
    for layer in range(LAYERS):
        one = slice(layer, layer + 1)
        before = jnp.zeros((24, 64), F32) + b1[one, :].astype(F32)
        for j in range(33):
            before = before + features[:, j : j + 1] * w1_rows[j][one]
        hidden = jnp.sin(before)
        slope[layer] = jnp.cos(before)
        raw = jnp.dot(
            hidden, w2[layer].astype(F32), precision=highest, preferred_element_type=F32
        )
        distance = lax.broadcasted_iota(jnp.int32, (24, 2 * D), 0).astype(F32)
        r = rate[one, :]
        wide_window = window[one, :]
        shaped = raw * jnp.exp(-wide_window * distance)
        loss = losses[one, :]
        table[layer] = shaped
        fp[layer] = shaped
        fp[layer, 16:17, :] = shaped[16:17] * loss
        fp[layer, 17:18, :] = r
        fp[layer, 18:24, :] = jnp.zeros((6, 2 * D), F32)
        rates[layer, 0:1, :] = wide_window
        rates[layer, 1:2, :] = r
        rates[layer, 2:3, :] = loss
        rates[layer, 3:8, :] = jnp.zeros((5, 2 * D), F32)
        square = jnp.concatenate([hidden, jnp.zeros((104, 64), F32)], axis=0)
        square = jnp.concatenate([square, jnp.zeros((128, 64), F32)], axis=1)
        turned[layer] = square.T[0:64]
        for k in range(3):
            sw[layer, k : k + 1, :] = short_rows[k][one]
        sw[layer, 3:4, :] = short_bias[one, :].astype(F32)
        sw[layer, 4:8, :] = jnp.zeros((4, 3 * D), F32)
        for i, vector in enumerate(vectors):
            outs[layer * 9 + i][...] = vector[one, :].astype(F32)
        outs[layer * 9 + 8][0:1, :] = r[:, 0:D]
        outs[layer * 9 + 8][1:2, :] = r[:, D : 2 * D]
        outs[layer * 9 + 8][2:8, :] = jnp.zeros((6, D), F32)
    own = offsets[...]
    offs[64:192, :] = jnp.broadcast_to(own, (128, LANES)).T
    start = offs[64:65, :]
    back = lax.broadcasted_iota(jnp.int32, (64, LANES), 0) - 64
    offs[0:64, :] = jnp.maximum(start + back, 0)
    offs[192:208, :] = jnp.zeros((16, LANES), jnp.int32)


def features_table():
    table = np.zeros((24, LANES), np.float32)
    table[: TAPS + 1, :33] = positions(TAPS + 1, 33)
    return table


class Prepared(typing.NamedTuple):
    fp: typing.Any
    sw: typing.Any
    table: typing.Any
    rates: typing.Any
    slope: typing.Any
    turned: typing.Any
    offs: typing.Any


def prepare(offsets, w):
    vectors = (
        w.ln1_gain,
        w.ln1_bias,
        w.in_bias,
        w.out_bias,
        w.ln2_gain,
        w.ln2_bias,
        w.fc1_bias,
        w.fc2_bias,
    )
    ins = (
        jnp.asarray(features_table()),
        jnp.sqrt(-jnp.expm1(-2.0 * w.decay_rate)),
        offsets,
        w.filter_w1.transpose(1, 0, 2),
        w.filter_b1,
        w.filter_w2,
        w.filter_window,
        w.decay_rate,
        w.short_weight.transpose(1, 0, 2),
        w.short_bias,
    ) + vectors
    outs = [
        ((LAYERS, 24, 2 * D), F32, FAR),
        ((LAYERS, 8, 3 * D), F32, FAR),
        ((LAYERS, 24, 2 * D), F32, FAR),
        ((LAYERS, 8, 2 * D), F32, FAR),
        ((LAYERS, 24, 64), F32, FAR),
        ((LAYERS, 64, LANES), F32, FAR),
        ((208, LANES), jnp.int32, FAR),
    ]
    sizes = [(1, vector.shape[1]) for vector in vectors] + [(8, D)]
    outs += [(size, F32) for _ in range(LAYERS) for size in sizes]
    made = run(prepare_kernel, [(NEAR if i == 1 else FAR, x) for i, x in enumerate(ins)], outs)
    return Prepared(*made[:7]), [Vectors(*made[7 + 9 * i : 16 + 9 * i]) for i in range(LAYERS)]


class Vectors(typing.NamedTuple):
    ln1_gain: typing.Any
    ln1_bias: typing.Any
    in_bias: typing.Any
    out_bias: typing.Any
    ln2_gain: typing.Any
    ln2_bias: typing.Any
    fc1_bias: typing.Any
    fc2_bias: typing.Any
    rates: typing.Any


class Params(typing.NamedTuple):
    ln1_gain: typing.Any
    ln1_bias: typing.Any
    in_weight: typing.Any
    in_bias: typing.Any
    short_weight: typing.Any
    short_bias: typing.Any
    filter_w1: typing.Any
    filter_b1: typing.Any
    filter_w2: typing.Any
    filter_window: typing.Any
    decay_rate: typing.Any
    out_weight: typing.Any
    out_bias: typing.Any
    ln2_gain: typing.Any
    ln2_bias: typing.Any
    fc1_weight: typing.Any
    fc1_bias: typing.Any
    fc2_weight: typing.Any
    fc2_bias: typing.Any


class Saved(typing.NamedTuple):
    stream: typing.Any
    normed: typing.Any
    proj: typing.Any
    gate1: typing.Any
    gate2: typing.Any
    vals: typing.Any
    yloc: typing.Any
    sloc: typing.Any
    pieces: typing.Any
    through: typing.Any
    inner: typing.Any
    outer: typing.Any
    conv2: typing.Any
    state2: typing.Any
    carry: typing.Any
    middle: typing.Any
    normed2: typing.Any
    act: typing.Any
    hidden: typing.Any


def wide(value):
    return value.astype(F32)


def rows_of(layer):
    return slice(192 - LENGTHS[layer], 208)


def forward_layer(layer, stream, where, p, made, v):
    length = LENGTHS[layer]
    normed = layer_norm(stream, v.ln1_gain, v.ln1_bias).astype(BF16)
    proj = (dot(normed, p.in_weight) + v.in_bias).astype(BF16)
    pad = (length + 16, LANES)
    offs = (FAR, made.offs, rows_of(layer))
    fp = (FAR, made.fp, layer)
    gate1, gate2, vals, yloc, sloc, summ = run(
        functools.partial(front_kernel, length),
        [(NEAR, proj), offs, (FAR, made.sw, layer), fp],
        [
            ((length, D), F32, FAR),
            ((length, D), F32, FAR),
            ((length, D), BF16, FAR),
            ((length, D), F32, FAR),
            ((length, D), F32, FAR),
            ((8, D), F32),
        ],
        [(pad, F32), (pad, F32), (pad, F32)],
    )
    near = [seq_shift(summ, True, i) for i in (1, 2, 3)]
    total, before, pieces = run(
        join_kernel,
        [(SCALARS, where), (NEAR, summ)] + [(NEAR, x) for x in near] + [(NEAR, v.rates)],
        [((8, D), F32)] * 3,
    )
    far = [seq_shift(total, False, i) for i in (1, 2, 3)]
    inner, outer, conv2, state2, carry, through = run(
        functools.partial(rest_kernel, length),
        [(SCALARS, where), (NEAR, before)]
        + [(NEAR, x) for x in far]
        + [(FAR, gate1), (FAR, gate2), (FAR, yloc), offs, fp],
        [
            ((length, D), BF16, FAR),
            ((length - 32, D), BF16),
            ((length - 32, D), F32, FAR),
            ((length - 32, D), F32, FAR),
            ((8, D), F32, FAR),
            ((8, D), F32, FAR),
        ],
        [((length, LANES), F32), (pad, F32)],
    )
    middle = stream[32:] + dot(outer, p.out_weight) + v.out_bias
    normed2 = layer_norm(middle, v.ln2_gain, v.ln2_bias).astype(BF16)
    act = dot(normed2, p.fc1_weight) + v.fc1_bias
    hidden = jax.nn.gelu(act).astype(BF16)
    result = middle + dot(hidden, p.fc2_weight) + v.fc2_bias
    saved = Saved(
        stream=stream,
        normed=normed,
        proj=proj,
        gate1=gate1,
        gate2=gate2,
        vals=vals,
        yloc=yloc,
        sloc=sloc,
        pieces=pieces,
        through=through,
        inner=inner,
        outer=outer,
        conv2=conv2,
        state2=state2,
        carry=carry,
        middle=middle,
        normed2=normed2,
        act=act,
        hidden=hidden,
    )
    return result, saved


def weights_kernel(jobs, split, aliased, small, *refs):
    refs = list(refs)
    where = refs.pop(0)
    pairs = [(refs.pop(0), refs.pop(0)) for _ in jobs]
    extra = refs.pop(0) if small is not None else None
    outs_count = 2 if split else 1
    if aliased:
        refs = refs[outs_count:]
    outs = refs[:outs_count]
    wide_buf, tall_buf, sems, small_sems = refs[outs_count:]
    me = where[2]

    def place(core, parts, side, chunk, row, rows):
        if split and len(outs[core].shape) == 4:
            return outs[core].at[chunk, parts, pl.ds(row, rows)]
        if split:
            return outs[core].at[side, chunk, parts, pl.ds(row, rows)]
        return outs[0].at[parts, core, side, chunk, pl.ds(row, rows)]

    def mine(core):
        return me ^ core if split else core

    every = pl.ds(0, 4)
    waiting = {}
    started = []
    if small is not None:
        for core in range(2):
            copy = pltpu.make_async_copy(
                extra.at[:, mine(core)], place(core, every, 0, 3, small, 64), small_sems.at[core]
            )
            copy.start()
            started.append(copy)
    step = 0
    for (a, g), blocks in zip(pairs, jobs):
        tall = a.shape[1] > D
        turned = None
        for index, copies_of in enumerate(blocks):
            if tall or turned is None:
                left = index * D if tall else 0
                turned = a[:, left : left + D].T
            right = 0 if tall else index * D
            slot = step % 2
            for copy in waiting.pop(slot, ()):
                copy.wait()
            w = jnp.dot(turned, g[:, right : right + D], preferred_element_type=F32).astype(BF16)
            copies = []
            if tall:
                tall_buf[slot] = w.reshape(2, 4, 96, D)
            else:
                wide_buf[slot] = w.reshape(4, 2, 96, D)
            for first, rows, side, chunk, row in copies_of:
                for core in range(2):
                    if tall:
                        source = tall_buf.at[slot, mine(core)]
                        target = place(core, index, side, every, row, 96)
                    else:
                        source = wide_buf.at[slot, :, mine(core), pl.ds(first, rows)]
                        target = place(core, every, side, chunk, row, rows)
                    sem = sems.at[slot, len(copies)]
                    copies.append(pltpu.make_async_copy(source, target, sem))
            for copy in copies:
                copy.start()
            waiting[slot] = copies
            step += 1
    for copies in waiting.values():
        started.extend(copies)
    for copy in started:
        copy.wait()


def weight_grads(where, pairs, jobs, rows, split, small=None, extra=None, onto=None):
    shape = (2, 4, 4, rows, D) if split else (4, 2, 2, 4, rows, D)
    if len(pairs) == 1:
        shape = (4, 4, rows, D)
    outs = [pltpu.HBM(shape, BF16)] * (2 if split else 1)
    operands = [where] + [x for pair in pairs for x in pair]
    in_specs = [smem()] + [vmem()] * (2 * len(pairs))
    if extra is not None:
        operands.append(extra)
        in_specs.append(vmem())
    aliases = {}
    if onto is not None:
        aliases = {len(operands) + i: i for i in range(len(outs))}
        operands += [in_hbm(x) for x in onto]
        in_specs += [pl.BlockSpec(memory_space=pltpu.HBM)] * len(outs)
    tokens = pairs[0][0].shape[0]
    blocks = sum(len(job) for job in jobs)
    return pl.pallas_call(
        functools.partial(weights_kernel, jobs, split, onto is not None, small),
        out_shape=outs,
        in_specs=in_specs,
        out_specs=[pl.BlockSpec(memory_space=pltpu.HBM)] * len(outs),
        input_output_aliases=aliases,
        scratch_shapes=[
            pltpu.VMEM((2, 4, 2, 96, D), BF16),
            pltpu.VMEM((2, 2, 4, 96, D), BF16),
            pltpu.SemaphoreType.DMA((2, 4)),
            pltpu.SemaphoreType.DMA((2,)),
        ],
        compiler_params=pltpu.CompilerParams(vmem_limit_bytes=VMEM_LIMIT),
        cost_estimate=pl.CostEstimate(
            flops=2 * 256 * D * D * blocks, bytes_accessed=2 * D * D * blocks, transcendentals=0
        ),
    )(*operands)


def ff_jobs(row):
    fc1 = tuple(((0, 96, 0, chunk, row),) for chunk in range(4))
    fc2 = tuple(((0, 96, 1, None, row),) for _ in range(4))
    return fc1, fc2


def mix_jobs(row):
    def low(side):
        return ((0, 64, side, 0, row), (64, 32, side, 1, row))

    def high(side):
        return ((0, 32, side, 1, row + 32), (32, 64, side, 2, row))

    return (low(1), high(1), low(0)), (high(0),)


def small_kernel(*refs):
    vectors = refs[:6]
    fc1_bias, columns, filt, table, rates, w2, turned, slope, out, buf, draw, narrow = refs[6:]
    window, rate, loss = rates[0:1, :], rates[1:2, :], rates[2:3, :]
    far = filt[TAPS : TAPS + 1, :]
    dwindow = jnp.zeros((1, 2 * D), F32)
    for k in range(TAPS + 1):
        d = filt[k : k + 1, :] * (loss if k == TAPS else 1.0)
        dwindow = dwindow - float(k) * table[k : k + 1, :] * d
        draw[k : k + 1, :] = d * jnp.exp(-window * float(k))
    draw[17:18, :] = dwindow
    draw[18:19, :] = (
        far * table[TAPS : TAPS + 1, :] * jnp.exp(-2.0 * rate) / loss
        - filt[TAPS + 1 : TAPS + 2, :] * jnp.exp(-rate)
    )
    draw[19:24, :] = jnp.zeros((5, 2 * D), F32)
    dhidden = lax.dot_general(
        draw[...],
        w2[...].astype(F32),
        (((1,), (1,)), ((), ())),
        precision=highest,
        preferred_element_type=F32,
    )
    dbefore = dhidden * slope[...]
    dw1 = jnp.zeros((40, 64), F32)
    for k in range(TAPS + 1):
        dw1 = dw1 + turned[:, k : k + 1] * dbefore[k : k + 1, :]
    narrow[...] = dw1
    buf[...] = jnp.zeros((64, D), F32)

    def columns_of(value, part, width):
        return pltpu.roll(value, (value.shape[1] - part * width) % value.shape[1], 1)[:, :width]

    pad64 = jnp.zeros((40, 64), F32)
    tall = jnp.concatenate([narrow[...], pad64], axis=1)
    flat = jnp.concatenate([v[...] for v in vectors] + [jnp.zeros((2, D), F32)], axis=0)
    for part in range(8):
        buf[0:6, 0:96] = columns_of(flat, part, 96)[0:6]
        buf[6:7, 0:384] = fc1_bias[:, part * 384 : (part + 1) * 384]
        buf[7:12, 0:288] = columns_of(columns[...], part, 288)[0:5]
        buf[12:31, 0:192] = columns_of(draw[...], part, 192)[0:19]
        mine = columns_of(tall, part, 8)
        buf[31:64, 0:8] = mine[0:33]
        buf[6:7, 384:392] = mine[33:34]
        out[part // 2, part % 2] = buf[...].astype(BF16)


def turned_features():
    table = np.zeros((40, LANES), np.float32)
    table[:33, : TAPS + 1] = positions(TAPS + 1, 33).T
    table[33, : TAPS + 1] = 1.0
    return table


def backward_layer(layer, grad, where, p, made, v, s, beside=None):
    length = LENGTHS[layer]
    first = layer == 0
    offs = (FAR, made.offs, rows_of(layer))
    fp = (FAR, made.fp, layer)
    grad_fc2_bias = jnp.sum(grad, axis=0)
    grad_low = grad.astype(BF16)
    dhidden = dot_t(grad_low, p.fc2_weight)
    dact = jax.vjp(jax.nn.gelu, s.act)[1](dhidden)[0]
    grad_fc1_bias = jnp.sum(dact, axis=0)
    dact_low = dact.astype(BF16)
    dnormed2 = dot_t(dact_low, p.fc1_weight)
    dmiddle, grad_ln2_gain, grad_ln2_bias = layer_norm_back(s.middle, v.ln2_gain, dnormed2)
    dmiddle = dmiddle + grad
    grad_out_bias = jnp.sum(dmiddle, axis=0)
    dmiddle_low = dmiddle.astype(BF16)
    dout = dot_t(dmiddle_low, p.out_weight)
    pad = (length + 16, LANES)
    dinner, sums, direct = run(
        functools.partial(back_kernel, length),
        [
            (NEAR, dout),
            (FAR, s.gate1),
            (FAR, s.gate2),
            (FAR, s.state2),
            (FAR, s.inner),
            offs,
            fp,
        ],
        [((length, D), F32, FAR), ((24, D), F32, FAR), ((8, D), F32)],
        [(pad, F32), (pad, F32), (pad, F32), ((length, LANES), F32)],
    )
    near = [seq_shift(direct, True, i) for i in (1, 2, 3)]
    ff = weight_grads(
        where, [(s.normed2, dact_low), (s.hidden, grad_low)], ff_jobs(0), 96, False
    )[0]
    near, ff = lax.optimization_barrier((near, ff))
    ff = lax.psum_scatter(ff.reshape(8, 2, 4, 96, D), DP, scatter_dimension=0, tiled=False)
    total, after = run(
        join_back_kernel,
        [(SCALARS, where), (NEAR, direct)]
        + [(NEAR, x) for x in near]
        + [(NEAR, s.pieces), (NEAR, v.rates)],
        [((8, D), F32)] * 2,
    )
    far = [seq_shift(total, False, i) for i in (1, 2, 3)]
    if first:
        beside = [add(beside[0][side], beside[1][side]) for side in range(2)]
    far, beside = lax.optimization_barrier((far, beside))
    dproj, colsums, filt = run(
        functools.partial(end_kernel, length),
        [(SCALARS, where), (NEAR, after)]
        + [(NEAR, x) for x in far]
        + [
            (FAR, s.through),
            (FAR, dinner),
            (NEAR, dout),
            (FAR, s.conv2),
            (FAR, s.gate1),
            (FAR, s.yloc),
            (FAR, s.sloc),
            (FAR, s.vals),
            (FAR, s.carry),
            (FAR, s.proj),
            offs,
            (FAR, made.sw, layer),
            fp,
            (FAR, sums),
        ],
        [((length, 3 * D), BF16), ((8, 3 * D), F32), ((24, 2 * D), F32)],
        [(pad, F32)] * 5,
    )
    pairs = [(s.normed, dproj), (s.outer, dmiddle_low)]
    if first:
        mix = weight_grads(where, pairs, mix_jobs(0), 64, True)
        dproj, mix = lax.optimization_barrier((dproj, mix))
        mix_came = swap(mix[1], DP, 1)
    dnormed = dot_t(dproj, p.in_weight)
    dstream, grad_ln1_gain, grad_ln1_bias = layer_norm_back(s.stream, v.ln1_gain, dnormed)
    dstream = dstream + jnp.concatenate([jnp.zeros((32, D), F32), dmiddle], axis=0)
    vectors = (
        grad_ln1_gain,
        grad_ln1_bias,
        grad_out_bias,
        grad_ln2_gain,
        grad_ln2_bias,
        grad_fc2_bias,
        grad_fc1_bias,
    )
    small = run(
        small_kernel,
        [(NEAR, vector.reshape(1, -1)) for vector in vectors]
        + [
            (NEAR, colsums),
            (NEAR, filt),
            (FAR, made.table, layer),
            (FAR, made.rates, layer),
            (FAR, p.filter_w2, layer),
            (FAR, jnp.asarray(turned_features())),
            (FAR, made.slope, layer),
        ],
        [((4, 2, 64, D), BF16)],
        [((64, D), F32), ((24, 2 * D), F32), ((40, 64), F32)],
    )[0]
    if first:
        own = take(small, where[2], 1, 1)
        other = swap(take(small, 1 - where[2], 1, 1), DP, 1)
        mix = [
            jnp.concatenate([add(mix[0][side], mix_came[side]), beside[side]], axis=2)
            for side in range(2)
        ]
        mix[0] = lax.dynamic_update_slice(mix[0], add(own, other)[None], (3, 0, 0, 0))
    else:
        mix = weight_grads(where, pairs, mix_jobs(0), 64, True, 0, small)
        mix = (mix[0], swap(mix[1], DP, 1))
    return dstream, ff, mix, beside


def add(*values):
    total = wide(values[0])
    for value in values[1:]:
        total = total + wide(value)
    return total.astype(BF16)


class Ring(typing.NamedTuple):
    me: typing.Any
    shift: typing.Any


def take(block, index, axis=0, bits=3):
    return lax.dynamic_index_in_dim(block, index & bits, axis, keepdims=False)


def scatter_direct(ring, block, axis):
    parts = [take(block, ring.me, axis)]
    parts += [ring.shift(take(block, ring.me + i, axis), i) for i in (1, 2, 3)]
    return add(*parts)


def both_ways(ring, pair):
    return ring.shift(pair[0], 1), ring.shift(pair[1], 3)


def scatter_ring(ring, block, dim):
    far = take(block, ring.me + 2)
    half = far.shape[dim] // 2
    up, down = both_ways(
        ring,
        (
            lax.slice_in_dim(far, 0, half, axis=dim),
            lax.slice_in_dim(far, half, 2 * half, axis=dim),
        ),
    )
    none = jnp.zeros_like(up)
    up = jnp.concatenate([up, none], axis=dim)
    down = jnp.concatenate([none, down], axis=dim)
    came = both_ways(
        ring, (add(take(block, ring.me + 1), up), add(take(block, ring.me - 1), down))
    )
    return add(take(block, ring.me), *came)


def gather_direct(ring, block):
    return jnp.stack([block] + [ring.shift(block, i) for i in (1, 2, 3)])


def gather_ring(ring, block):
    half = block.shape[0] // 2
    before = ring.shift(block, 1)
    after = ring.shift(block, 3)
    return block, before, after, ring.shift(before[:half], 1), ring.shift(after[half:], 3)


def unpack_kernel(where, turned, *refs):
    sides = (refs[0:5], refs[5:10])
    inw, outw, fc1, fc2 = refs[10:14]
    small = refs[14:29]
    rows, mixed = refs[29:]
    for side, (own, before, after, far_low, far_high) in enumerate(sides):
        ring = where[side]
        other = where[1 - side]
        for distance, pieces in (
            (0, ((own, 0, 4),)),
            (1, ((before, 0, 4),)),
            (3, ((after, 0, 4),)),
            (2, ((far_low, 0, 2), (far_high, 2, 4))),
        ):
            chunk = (ring - distance) & 3
            for ref, low, high in pieces:
                for i in range(low, high):
                    at = pl.multiple_of(((other - i) & 3) * 40, 8)
                    for layer in range(LAYERS):
                        rows[layer, pl.ds(at, 40), :] = ref[i - low, layer].astype(F32)
            for layer in range(LAYERS):
                if side == 0:
                    fc1[layer, :, pl.ds(pl.multiple_of(chunk * D, D), D)] = rows[layer, 0:96, :]
                else:
                    fc2[layer, pl.ds(pl.multiple_of(chunk * 96, 96), 96), :] = rows[layer, 0:96, :]
                mixed[side, layer, pl.ds(pl.multiple_of(chunk * 64, 64), 64), :] = rows[
                    layer, 96:160, :
                ]
    (
        ln1_gain,
        ln1_bias,
        out_bias,
        ln2_gain,
        ln2_bias,
        fc2_bias,
        fc1_bias,
        in_bias,
        short_weight,
        short_bias,
        filter_w1,
        filter_b1,
        filter_w2,
        window,
        decay,
    ) = small
    for layer in range(LAYERS):
        inw[layer, :, 0:D] = mixed[1, layer, 0:96, :]
        inw[layer, :, D : 2 * D] = mixed[1, layer, 96:192, :]
        inw[layer, :, 2 * D : 3 * D] = mixed[0, layer, 0:96, :]
        outw[layer] = mixed[0, layer, 96:192, :]
        one = pl.ds(layer, 1)
        for row, out in enumerate((ln1_gain, ln1_bias, out_bias, ln2_gain, ln2_bias, fc2_bias)):
            out[one, :] = mixed[0, layer, 192 + row : 193 + row, 0:96]
        fc1_bias[one, :] = mixed[0, layer, 198:199, 0:384]
        filter_b1[one, :] = mixed[0, layer, 198:199, 384:392]
        in_bias[one, :] = mixed[0, layer, 199:200, 0:288]
        for k in range(3):
            short_weight[k, one, :] = mixed[0, layer, 200 + k : 201 + k, 0:288]
        short_bias[one, :] = mixed[0, layer, 203:204, 0:288]
        window[one, :] = mixed[0, layer, 221:222, 0:192]
        decay[one, :] = mixed[0, layer, 222:223, 0:192]
        filter_w1[layer] = mixed[0, layer, 223:256, 0:8]
        total = jnp.zeros((64, 192), F32)
        for k in range(TAPS + 1):
            draw = mixed[0, layer, 204 + k : 205 + k, 0:192]
            total = total + turned[layer, :, k : k + 1] * draw
        filter_w2[layer] = total


def side_rings(where):
    return (
        Ring(where[0], lambda block, i: seq_shift(block, False, i)),
        Ring(where[1], lambda block, i: seq_shift(block, True, i)),
    )


def reduce_grads(where, turned, ff, mix):
    rings = side_rings(where)
    y_ring = Ring(where[3], part_shift)
    sides = [scatter_ring(ring, mix[side], 1) for side, ring in enumerate(rings)]
    sides, ff = lax.optimization_barrier((sides, ff))
    mix = scatter_ring(y_ring, jnp.stack(sides, axis=1), 0).reshape(2, LAYERS, 64, D)
    sums = []
    for side, ring in enumerate(rings):
        block = jnp.concatenate([ff[0][side], ff[1][side]], axis=1)
        sums.append(scatter_direct(ring, block, 0).reshape(LAYERS, 96, D))
    pieces = []
    for side in range(2):
        other = rings[1 - side]
        two = jnp.concatenate([sums[side], mix[side]], axis=1).reshape(2, 4, 40, D)
        own = scatter_direct(other, two, 1)
        pieces.extend(gather_ring(rings[side], gather_direct(other, own)))
    shapes = [(LAYERS, 96, 3 * D), (LAYERS, 96, D), (LAYERS, 96, FF), (LAYERS, 384, D)]
    shapes += [(LAYERS, 96)] * 6 + [(LAYERS, 384), (LAYERS, 288), (3, LAYERS, 288), (LAYERS, 288)]
    shapes += [(LAYERS, 33, 8), (LAYERS, 8), (LAYERS, 64, 192)] + [(LAYERS, 192)] * 2
    return pl.pallas_call(
        unpack_kernel,
        out_shape=[jax.ShapeDtypeStruct(shape, F32) for shape in shapes],
        in_specs=[smem()] + [vmem()] * 11,
        out_specs=[vmem()] * len(shapes),
        scratch_shapes=[
            pltpu.VMEM((LAYERS, 160, D), F32),
            pltpu.VMEM((2, LAYERS, 256, D), F32),
        ],
        compiler_params=pltpu.CompilerParams(vmem_limit_bytes=24 * 1024 * 1024),
    )(where, turned, *pieces)


def body(tokens, out_grad, offsets, *weights):
    part = lax.axis_index(DP).astype(jnp.int32)
    place = lax.axis_index(SEQ).astype(jnp.int32)
    where = jnp.stack([place // 4, place % 4, part % 2, part // 2])
    weights = Params(*weights)
    made, vectors = prepare(offsets, weights)
    params = [
        weights._replace(
            in_weight=weights.in_weight[layer],
            out_weight=weights.out_weight[layer],
            fc1_weight=weights.fc1_weight[layer],
            fc2_weight=weights.fc2_weight[layer],
        )
        for layer in range(LAYERS)
    ]
    own = tokens[0]
    halo = from_left(own[BLK - 64 :])
    stream = jnp.concatenate([halo, own], axis=0).astype(F32)
    saved = []
    for layer in range(LAYERS):
        stream, kept = forward_layer(layer, stream, where, params[layer], made, vectors[layer])
        saved.append(kept)
    mixed = stream.astype(BF16)[None]
    grad = out_grad[0].astype(F32)
    grad, ff_last, mix_last, mixed = backward_layer(
        1, grad, where, params[1], made, vectors[1], saved[1], mixed
    )
    grad, kept = lax.optimization_barrier((grad, mix_last[0]))
    grad, ff_first, mix_first, _ = backward_layer(
        0, grad, where, params[0], made, vectors[0], saved[0], (kept, mix_last[1])
    )
    returned = from_right(grad[:64])
    input_grad = jnp.concatenate([grad[64:128], grad[128:] + returned], axis=0)[None]
    found = reduce_grads(where, made.turned, (ff_first, ff_last), mix_first)
    grads = Params(
        in_weight=found[0],
        out_weight=found[1],
        fc1_weight=found[2],
        fc2_weight=found[3],
        ln1_gain=found[4],
        ln1_bias=found[5],
        out_bias=found[6],
        ln2_gain=found[7],
        ln2_bias=found[8],
        fc2_bias=found[9],
        fc1_bias=found[10],
        in_bias=found[11],
        short_weight=found[12].transpose(1, 0, 2),
        short_bias=found[13],
        filter_w1=found[14],
        filter_b1=found[15],
        filter_w2=found[16],
        filter_window=found[17],
        decay_rate=found[18],
    )
    return (mixed, input_grad) + tuple(grads)


def solution(mesh):
    block = P(DP, SEQ, None)
    rows = P(None, DP, None)
    columns = P(None, None, DP)
    vector = P(None, DP)
    outs = Params(*([vector] * len(Params._fields)))._replace(
        in_weight=rows,
        out_weight=rows,
        fc1_weight=rows,
        fc2_weight=rows,
        short_weight=columns,
        filter_w1=columns,
        filter_w2=columns,
    )
    return jax.shard_map(
        body,
        mesh=mesh,
        in_specs=(block, block, P(DP, SEQ)) + (P(),) * len(outs),
        out_specs=(block, block) + tuple(outs),
        check_vma=False,
    )
```

```python
import functools
import math
import typing

import jax
import jax.numpy as jnp
import numpy as np
from jax import lax
from jax.experimental import pallas as pl
from jax.experimental.pallas import tpu as pltpu
from jax.sharding import PartitionSpec as P

SEQ = "seq"
DP = "dp"
TAPS = 16
LAYERS = 2
D = 768
FF = 3072
BLK = 128
LANES = 128
TILES = D // LANES
F32 = jnp.float32
BF16 = jnp.bfloat16
highest = lax.Precision.HIGHEST

LENGTHS = (192, 160)

VMEM_LIMIT = 14 * 1024 * 1024


def in_hbm(value):
    return pltpu.with_memory_space_constraint(value, pltpu.HBM)


def vmem():
    return pl.BlockSpec(memory_space=pltpu.VMEM)


def smem():
    return pl.BlockSpec(memory_space=pltpu.SMEM)


NEAR, SCALARS, FAR = range(3)


def halves_of(shape, source, target):
    out = []
    for half in range(2):
        pairs = []
        for block in range(shape[1] // D):
            cols = pl.ds(block * D + half * (D // 2), D // 2)
            pairs.append((source.at[:, cols], target.at[:, cols]))
        out.append(pairs)
    return out


def run(kernel, ins, outs, scratch=(), limit=VMEM_LIMIT, tiled=False):
    ins = [(item + (None,))[:3] for item in ins]
    outs = [(item + (NEAR,))[:3] for item in outs]
    far_ins = [i for i, item in enumerate(ins) if item[0] == FAR]
    far_outs = [i for i, item in enumerate(outs) if item[2] == FAR]

    def part(item):
        if item[2] is None:
            return item[1].shape
        return jax.eval_shape(lambda x: x[item[2]], item[1]).shape

    in_shapes = [part(ins[i]) for i in far_ins]
    buffers = [pltpu.VMEM(shape, ins[i][1].dtype) for shape, i in zip(in_shapes, far_ins)]
    buffers += [pltpu.VMEM(outs[i][0], outs[i][1]) for i in far_outs]
    sem_count = 6 * len(buffers) + 1

    def big(shape):
        return tiled and len(shape) == 2 and shape[0] >= 96 and shape[1] % D == 0

    def whole(*refs):
        in_refs = list(refs[: len(ins)])
        out_refs = list(refs[len(ins) : len(ins) + len(outs)])
        rest = refs[len(ins) + len(outs) :]
        stores = rest[: len(buffers)]
        sems = rest[-1]
        used = 0
        arriving = ([], [])
        leaving = ([], [])

        def plan(shape, source, target, queues, small):
            nonlocal used
            groups = halves_of(shape, source, target) if big(shape) else [[], []]
            if not big(shape):
                groups[small] = [(source, target)]
            for queue, group in zip(queues, groups):
                for pair in group:
                    queue.append(pltpu.make_async_copy(*pair, sems.at[used]))
                    used += 1

        for n, i in enumerate(far_ins):
            index = ins[i][2]
            if isinstance(index, slice):
                index = pl.ds(index.start, index.stop - index.start)
            source = in_refs[i] if index is None else in_refs[i].at[index]
            plan(in_shapes[n], source, stores[n], arriving, 0)
            in_refs[i] = stores[n]
        for n, i in enumerate(far_outs, len(far_ins)):
            plan(outs[i][0], stores[n], out_refs[i], leaving, 1)
            out_refs[i] = stores[n]
        for queue in arriving:
            for copy in queue:
                copy.start()

        def arrive(half):
            for copy in arriving[half]:
                copy.wait()

        def leave(half):
            for copy in leaving[half]:
                copy.start()

        args = (*in_refs, *out_refs, *rest[len(buffers) : -1])
        if tiled:
            kernel(arrive, leave, *args)
        else:
            arrive(0)
            kernel(*args)
            leave(1)
        for queue in leaving:
            for copy in queue:
                copy.wait()

    spaces = {NEAR: pltpu.VMEM, SCALARS: pltpu.SMEM, FAR: pltpu.HBM}
    return pl.pallas_call(
        whole,
        out_shape=[
            pltpu.HBM(shape, dtype) if kind == FAR else jax.ShapeDtypeStruct(shape, dtype)
            for shape, dtype, kind in outs
        ],
        in_specs=[pl.BlockSpec(memory_space=spaces[item[0]]) for item in ins],
        out_specs=[pl.BlockSpec(memory_space=spaces[item[2]]) for item in outs],
        scratch_shapes=buffers
        + [pltpu.VMEM(shape, dtype) for shape, dtype in scratch]
        + [pltpu.SemaphoreType.DMA((sem_count,))],
        compiler_params=pltpu.CompilerParams(vmem_limit_bytes=limit),
    )(*(in_hbm(x) if kind == FAR else x for kind, x, _ in ins))


def tile_loop(arrive, leave, tile):
    for half in range(2):
        arrive(half)
        lax.fori_loop(half * (TILES // 2), (half + 1) * (TILES // 2), tile, 0)
        leave(half)


def rows_iota(start, count):
    return lax.broadcasted_iota(jnp.int32, (count, LANES), 0) + start


def chunks(start, stop):
    half = (stop - start) // 16 * 8
    return ((start, start + half), (start + half, stop))


def keep(mask, value):
    return jnp.where(mask, value, 0.0)


def powers(rate, exponent):
    return jnp.exp(-rate * exponent.astype(F32))


def scan_forward(src, offs, dst, rate, start, stop, base_src, base_dst):
    lane = lax.broadcasted_iota(jnp.int32, (8, LANES), 0)
    r1 = jnp.exp(-rate)
    r2 = r1 * r1
    r4 = r2 * r2
    climb = powers(rate, lane + 1)
    carry = None
    for row in range(start, stop, 8):
        o = offs[row : row + 8, :]
        reach = jnp.minimum(o, lane)
        y = src[base_src + row : base_src + row + 8, :]
        y = y + keep(reach >= 1, pltpu.roll(y, 1, 0) * r1)
        y = y + keep(reach >= 2, pltpu.roll(y, 2, 0) * r2)
        y = y + keep(reach >= 4, pltpu.roll(y, 4, 0) * r4)
        if carry is not None:
            y = y + keep(o >= lane + 1, climb * carry)
        dst[base_dst + row : base_dst + row + 8, :] = y
        carry = jnp.broadcast_to(y[7:8, :], (8, LANES))


def scan_backward(src, offs, dst, rate, start, stop, base_src, base_dst):
    lane = lax.broadcasted_iota(jnp.int32, (8, LANES), 0)
    r1 = jnp.exp(-rate)
    r2 = r1 * r1
    r4 = r2 * r2
    climb = powers(rate, 8 - lane)
    carry = None
    ahead = None
    for row in range(stop - 8, start - 1, -8):
        o = offs[row : row + 8, :]
        reach = jnp.minimum(o, lane)
        y = src[base_src + row : base_src + row + 8, :]
        y = y + pltpu.roll(keep(reach >= 1, y * r1), 7, 0)
        y = y + pltpu.roll(keep(reach >= 2, y * r2), 6, 0)
        y = y + pltpu.roll(keep(reach >= 4, y * r4), 4, 0)
        if carry is not None:
            y = y + keep(ahead >= 8 - lane, climb * carry)
        dst[base_dst + row : base_dst + row + 8, :] = keep(o > 0, y)
        carry = jnp.broadcast_to(y[0:1, :], (8, LANES))
        ahead = jnp.broadcast_to(o[0:1, :], (8, LANES))


def front_kernel(
    length, arrive, leave, proj, offs, sw, fp, gate1, gate2, vals, yloc, sloc, summ, ps, vs, ss
):
    last = length - 1
    zeros16 = jnp.zeros((16, LANES), F32)

    def tile(c, carry):
        col = pl.multiple_of(c * LANES, LANES)
        one = pl.ds(col, LANES)
        two = pl.ds(pl.multiple_of(col + D, LANES), LANES)
        ps[0:16, :] = zeros16
        vs[0:16, :] = zeros16
        ss[0:16, :] = zeros16
        ss[8:24, :] = zeros16

        def short(part):
            cols = pl.ds(pl.multiple_of(col + part * D, LANES), LANES)
            ps[16 : 16 + length, :] = proj[:, cols].astype(F32)
            w0, w1, w2, bias = (sw[i : i + 1, cols] for i in range(4))
            out = []
            for lo, hi in chunks(0, length):
                o = offs[lo:hi, :]
                out.append(
                    bias
                    + w0 * ps[16 + lo : 16 + hi, :]
                    + w1 * keep(o >= 1, ps[15 + lo : 15 + hi, :])
                    + w2 * keep(o >= 2, ps[14 + lo : 14 + hi, :])
                )
            return jnp.concatenate(out, axis=0)

        gate1[:, one] = short(0)
        gate2[:, one] = short(1)
        value = short(2).astype(BF16)
        vals[:, one] = value
        vs[16 : 16 + length, :] = value.astype(F32)
        rate1 = fp[17:18, one]
        rate2 = fp[17:18, two]
        tail1 = fp[16:17, one]
        scan_forward(vs, offs, ss, rate1, 16, length, 16, 8)
        sloc[:, one] = ss[8 : 8 + length, :]
        total_a = jnp.zeros((8, LANES), F32)
        total_b = jnp.zeros((8, LANES), F32)
        near = jnp.broadcast_to(offs[last : last + 1, :], (8, LANES))
        for lo, hi in chunks(16, length):
            o = offs[lo:hi, :]
            acc = keep(o > 0, ss[7 + lo : 7 + hi, :]) * tail1
            for k in range(TAPS):
                v = vs[16 + lo - k : 16 + hi - k, :]
                acc = acc + keep(o >= k, v) * fp[k : k + 1, one]
            yloc[lo:hi, one] = acc
        for lo in range(32, 160, 8):
            e = rows_iota(lo, 8)
            o = offs[lo : lo + 8, :]
            weight = keep(near >= last - e, powers(rate2, 159 - e)) * gate1[lo : lo + 8, one]
            total_a = total_a + weight * yloc[lo : lo + 8, one]
            total_b = total_b + weight * keep(o >= e - 15, powers(rate1, e - 16))
        end1 = keep(near[0:1, :] >= last - 143, ss[8 + 143 : 8 + 144, :])
        summ[0:1, one] = end1
        summ[1:2, one] = jnp.sum(total_a, axis=0, keepdims=True)
        summ[2:3, one] = jnp.sum(total_b, axis=0, keepdims=True) * tail1
        summ[3:8, one] = jnp.zeros((5, LANES), F32)
        return carry

    tile_loop(arrive, leave, tile)


def pick(values, index):
    out = values[0]
    for i in range(1, len(values)):
        out = jnp.where(index == i, values[i], out)
    return out


def join_kernel(where, own, r1, r2, r3, rates, total, before, pieces):
    z = where[1]
    parts = (own[...], r1[...], r2[...], r3[...])
    rate1, rate2 = rates[0:1, :], rates[1:2, :]
    f1 = jnp.exp(-rate1 * float(BLK))
    f2 = jnp.exp(-rate2 * float(BLK))
    e = jnp.zeros((1, D), F32)
    a = jnp.zeros((1, D), F32)
    b = jnp.zeros((1, D), F32)
    be, ba, bb = e, a, b
    reach = jnp.ones((1, D), F32)
    for i in range(4):
        here = pick(parts, (z - i) & 3)
        be = jnp.where(z == i, e, be)
        ba = jnp.where(z == i, a, ba)
        bb = jnp.where(z == i, b, bb)
        pieces[i : i + 1, :] = here[2:3, :]
        a = f2 * a + here[2:3, :] * e + here[1:2, :]
        b = f2 * b + here[2:3, :] * reach
        e = f1 * e + here[0:1, :]
        reach = reach * f1
    pad = jnp.zeros((5, D), F32)
    total[...] = jnp.concatenate([e, a, b, pad], axis=0)
    before[...] = jnp.concatenate([be, ba, bb, pad], axis=0)
    pieces[4:8, :] = jnp.zeros((4, D), F32)


def join_back_kernel(where, own, r1, r2, r3, pieces, rates, total, after):
    z = where[1]
    parts = (own[...], r1[...], r2[...], r3[...])
    rate1, rate2 = rates[0:1, :], rates[1:2, :]
    f1 = jnp.exp(-rate1 * float(BLK))
    f2 = jnp.exp(-rate2 * float(BLK))
    c1 = jnp.zeros((1, D), F32)
    c2 = jnp.zeros((1, D), F32)
    b = jnp.zeros((1, D), F32)
    s1, s2, sb = c1, c2, b
    reach = jnp.ones((1, D), F32)
    for i in (3, 2, 1, 0):
        here = pick(parts, (z - i) & 3)
        s1 = jnp.where(z == i, c1, s1)
        s2 = jnp.where(z == i, c2, s2)
        sb = jnp.where(z == i, b, sb)
        through = pieces[i : i + 1, :]
        c1 = f1 * c1 + through * c2 + here[0:1, :]
        c2 = f2 * c2 + here[1:2, :]
        b = f1 * b + through * reach
        reach = reach * f2
    total[...] = jnp.concatenate([c1, c2, jnp.zeros((6, D), F32)], axis=0)
    after[...] = jnp.concatenate([s1, s2, sb, jnp.zeros((5, D), F32)], axis=0)


def rest_kernel(
    length,
    arrive,
    leave,
    where,
    before,
    g1,
    g2,
    g3,
    gate1,
    gate2,
    yloc,
    offs,
    fp,
    inner,
    outer,
    conv2,
    state2,
    carry,
    through,
    ins,
    ss,
):
    x = where[0]
    z = where[1].astype(F32)
    for i, far in enumerate((g1, g2, g3)):
        through[i : i + 1, :] = far[2:3, :]
    through[3:8, :] = jnp.zeros((5, D), F32)
    zeros16 = jnp.zeros((16, LANES), F32)

    def tile(c, unused):
        col = pl.multiple_of(c * LANES, LANES)
        one = pl.ds(col, LANES)
        two = pl.ds(pl.multiple_of(col + D, LANES), LANES)
        rate1 = fp[17:18, one]
        rate2 = fp[17:18, two]
        tail1 = fp[16:17, one]
        tail2 = fp[16:17, two]
        f1 = jnp.exp(-rate1 * float(4 * BLK))
        f2 = jnp.exp(-rate2 * float(4 * BLK))
        parts = (g1[:, one], g1[:, one], g2[:, one], g3[:, one])
        c1 = jnp.zeros((1, LANES), F32)
        c2 = jnp.zeros((1, LANES), F32)
        for i in range(3):
            here = pick(parts, (x - i) & 3)
            n2 = f2 * c2 + here[1:2, :] + here[2:3, :] * c1
            n1 = f1 * c1 + here[0:1, :]
            c1 = jnp.where(i < x, n1, c1)
            c2 = jnp.where(i < x, n2, c2)
        c2 = jnp.exp(-rate2 * BLK * z) * c2 + before[1:2, one] + before[2:3, one] * c1
        c1 = jnp.exp(-rate1 * BLK * z) * c1 + before[0:1, one]
        carry[0:1, one] = c1
        carry[1:2, one] = c2
        carry[2:8, one] = jnp.zeros((6, LANES), F32)
        ins[0:16, :] = zeros16
        for lo in range(16, length, 16):
            e = rows_iota(lo, 16)
            o = offs[lo : lo + 16, :]
            y = yloc[lo : lo + 16, one] + keep(o >= e - 15, powers(rate1, e - 16)) * (tail1 * c1)
            low = (gate1[lo : lo + 16, one] * y).astype(BF16)
            inner[lo : lo + 16, one] = low
            ins[lo : lo + 16, :] = low.astype(F32)
        inner[0:16, one] = zeros16.astype(BF16)
        ss[0:40, :] = jnp.zeros((40, LANES), F32)
        scan_forward(ins, offs, ss, rate2, 32, length, 0, 8)
        for lo, hi in chunks(32, length):
            o = offs[lo:hi, :]
            e = rows_iota(lo, hi - lo)
            s = keep(o > 0, ss[7 + lo : 7 + hi, :])
            s = s + keep(o >= e - 31, powers(rate2, e - 32)) * c2
            state2[lo - 32 : hi - 32, one] = s
            acc = s * tail2
            for k in range(TAPS):
                acc = acc + keep(o >= k, ins[lo - k : hi - k, :]) * fp[k : k + 1, two]
            conv2[lo - 32 : hi - 32, one] = acc
        outer[:, one] = (gate2[32:length, one] * conv2[:, one]).astype(BF16)
        return unused

    tile_loop(arrive, leave, tile)


def back_kernel(
    length,
    arrive,
    leave,
    dout,
    gate1,
    gate2,
    state2,
    inner,
    offs,
    fp,
    dinner,
    sums,
    direct,
    xs,
    dys,
    qs,
    ins,
):
    last = length - 1
    zeros16 = jnp.zeros((16, LANES), F32)

    def tile(c, unused):
        col = pl.multiple_of(c * LANES, LANES)
        one = pl.ds(col, LANES)
        two = pl.ds(pl.multiple_of(col + D, LANES), LANES)
        rate1 = fp[17:18, one]
        rate2 = fp[17:18, two]
        tail1 = fp[16:17, one]
        tail2 = fp[16:17, two]
        dys[0:16, :] = zeros16
        dys[16:32, :] = zeros16
        dys[length : length + 16, :] = zeros16
        dy = dout[:, one] * gate2[32:length, one]
        dys[32:length, :] = dy
        xs[32:length, :] = dy * tail2
        qs[0:16, :] = zeros16
        qs[16:32, :] = zeros16
        qs[length : length + 8, :] = jnp.zeros((8, LANES), F32)
        scan_backward(xs, offs, qs, rate2, 32, length, 0, 0)
        direct[1:2, one] = qs[32:33, :]
        ins[...] = inner[:, one].astype(F32)
        near = offs[last : last + 1, :]
        tap_sums = [jnp.zeros((8, LANES), F32) for _ in range(TAPS)]
        d1 = jnp.zeros((8, LANES), F32)

        def fold(value):
            out = value[0:8]
            for i in range(8, value.shape[0], 8):
                out = out + value[i : i + 8]
            return out

        for lo, hi in chunks(16, length):
            acc = jnp.zeros((hi - lo, LANES), F32)
            v = ins[lo:hi, :]
            for k in range(TAPS):
                m = keep(offs[lo + k : hi + k, :] >= k, dys[lo + k : hi + k, :])
                acc = acc + m * fp[k : k + 1, two]
                tap_sums[k] = tap_sums[k] + fold(m * v)
            e = rows_iota(lo, hi - lo)
            acc = acc + keep(e >= 32, qs[lo + 1 : hi + 1, :])
            dinner[lo:hi, one] = acc
            o = offs[lo:hi, :]
            reach = keep(o >= e - 15, powers(rate1, e - 16))
            d1 = d1 + fold(reach * gate1[lo:hi, one] * acc)
        dinner[0:16, one] = zeros16
        direct[0:1, one] = jnp.sum(d1, axis=0, keepdims=True) * tail1
        direct[2:8, one] = jnp.zeros((6, LANES), F32)
        for k in range(TAPS):
            sums[k : k + 1, one] = jnp.sum(tap_sums[k], axis=0, keepdims=True)
        t_tail = jnp.zeros((8, LANES), F32)
        t_own = jnp.zeros((8, LANES), F32)
        t_next = jnp.zeros((8, LANES), F32)
        for lo in range(32, length, 8):
            s = state2[lo - 32 : lo - 24, one]
            t_tail = t_tail + s * dys[lo : lo + 8, :]
            t_own = t_own + s * qs[lo + 1 : lo + 9, :]
            if lo < 160:
                e = rows_iota(lo, 8)
                t_next = t_next + s * keep(near >= last - e, powers(rate2, 159 - e))
        sums[16:17, one] = jnp.sum(t_tail, axis=0, keepdims=True)
        sums[17:18, one] = jnp.sum(t_own, axis=0, keepdims=True)
        sums[18:19, one] = jnp.sum(t_next, axis=0, keepdims=True)
        sums[19:24, one] = jnp.zeros((5, LANES), F32)
        return unused

    tile_loop(arrive, leave, tile)


def end_kernel(
    length,
    arrive,
    leave,
    where,
    after,
    h1,
    h2,
    h3,
    through_of,
    dinner,
    dout,
    conv2,
    gate1,
    yloc,
    sloc,
    vals,
    carry,
    proj,
    offs,
    sw,
    fp,
    sums,
    dproj,
    colsums,
    filt,
    xs,
    dys,
    qs,
    ds,
    ss,
):
    last = length - 1
    x = where[0]
    later = (3 - where[1]).astype(F32)
    zeros16 = jnp.zeros((16, LANES), F32)

    def fold(value):
        out = value[0:8]
        for i in range(8, value.shape[0], 8):
            out = out + value[i : i + 8]
        return out

    def total(value):
        return jnp.sum(value, axis=0, keepdims=True)

    def tile(c, unused):
        col = pl.multiple_of(c * LANES, LANES)
        one = pl.ds(col, LANES)
        two = pl.ds(pl.multiple_of(col + D, LANES), LANES)
        three = pl.ds(pl.multiple_of(col + 2 * D, LANES), LANES)
        rate1 = fp[17:18, one]
        rate2 = fp[17:18, two]
        tail1 = fp[16:17, one]
        f1 = jnp.exp(-rate1 * float(4 * BLK))
        f2 = jnp.exp(-rate2 * float(4 * BLK))
        steps = (h1[:, one], h1[:, one], h2[:, one], h3[:, one])
        throughs = [through_of[i : i + 1, one] for i in (0, 0, 1, 2)]
        c1 = jnp.zeros((1, LANES), F32)
        c2 = jnp.zeros((1, LANES), F32)
        for i in (3, 2, 1):
            here = pick(steps, (x - i) & 3)
            through = pick(throughs, (x - i) & 3)
            n1 = f1 * c1 + through * c2 + here[0:1, :]
            n2 = f2 * c2 + here[1:2, :]
            c1 = jnp.where(i > x, n1, c1)
            c2 = jnp.where(i > x, n2, c2)
        c1 = jnp.exp(-rate1 * BLK * later) * c1 + after[0:1, one] + after[2:3, one] * c2
        c2 = jnp.exp(-rate2 * BLK * later) * c2 + after[1:2, one]
        near = offs[last : last + 1, :]
        carry1 = carry[0:1, one]

        for lo in (0, 16):
            dys[lo : lo + 16, :] = zeros16
            qs[lo : lo + 16, :] = zeros16
        dys[length : length + 16, :] = zeros16
        qs[length : length + 8, :] = jnp.zeros((8, LANES), F32)
        ds[0:16, :] = zeros16
        ds[length : length + 16, :] = zeros16
        ss[0:16, :] = zeros16
        ss[8 : 8 + length, :] = sloc[:, one]
        ss[8:24, :] = zeros16

        for lo in range(16, length, 8):
            e = rows_iota(lo, 8)
            o = offs[lo : lo + 8, :]
            d = dinner[lo : lo + 8, one]
            if 32 <= lo < 160:
                d = d + keep(near >= last - e, powers(rate2, 159 - e)) * c2
            conv1 = yloc[lo : lo + 8, one] + keep(o >= e - 15, powers(rate1, e - 16)) * (
                tail1 * carry1
            )
            ds[lo : lo + 8, :] = d * conv1
            dy = d * gate1[lo : lo + 8, one]
            dys[lo : lo + 8, :] = dy
            xs[lo : lo + 8, :] = dy * tail1

        def short_back(part, cols):
            w0, w1, w2 = (sw[i : i + 1, cols] for i in range(3))
            sums_of = [jnp.zeros((8, LANES), F32) for _ in range(5)]
            for lo in range(0, length, 16):
                hi = lo + 16
                p = proj[lo:hi, cols].astype(F32)
                m0 = ds[lo:hi, :]
                m1 = keep(offs[lo + 1 : hi + 1, :] >= 1, ds[lo + 1 : hi + 1, :])
                m2 = keep(offs[lo + 2 : hi + 2, :] >= 2, ds[lo + 2 : hi + 2, :])
                out = w0 * m0 + w1 * m1 + w2 * m2
                dproj[lo:hi, cols] = out.astype(BF16)
                for i, value in enumerate((out, p * m0, p * m1, p * m2, m0)):
                    sums_of[i] = sums_of[i] + fold(value)
            for i in range(5):
                colsums[i : i + 1, cols] = total(sums_of[i])
            colsums[5:8, cols] = jnp.zeros((3, LANES), F32)

        short_back(0, one)
        ds[16:32, :] = zeros16
        ds[32:length, :] = dout[:, one] * conv2[:, one]
        short_back(1, two)

        scan_backward(xs, offs, qs, rate1, 16, length, 0, 0)
        tap_sums = [jnp.zeros((8, LANES), F32) for _ in range(TAPS)]
        for lo, hi in chunks(0, length):
            v = vals[lo:hi, one].astype(F32)
            acc = jnp.zeros((hi - lo, LANES), F32)
            for k in range(TAPS):
                m = keep(offs[lo + k : hi + k, :] >= k, dys[lo + k : hi + k, :])
                acc = acc + m * fp[k : k + 1, one]
                tap_sums[k] = tap_sums[k] + fold(m * v)
            ds[lo:hi, :] = acc
        for k in range(TAPS):
            filt[k : k + 1, one] = total(tap_sums[k])
        t_tail = jnp.zeros((8, LANES), F32)
        t_retain = jnp.zeros((8, LANES), F32)
        for lo in range(16, length, 8):
            e = rows_iota(lo, 8)
            o = offs[lo : lo + 8, :]
            g = qs[lo + 1 : lo + 9, :]
            if lo < 144:
                g = g + keep(near >= last - e, powers(rate1, 143 - e)) * c1
            s = keep(o > 0, ss[lo + 7 : lo + 15, :]) + keep(
                o >= e - 15, powers(rate1, e - 16)
            ) * carry1
            t_tail = t_tail + s * dys[lo : lo + 8, :]
            t_retain = t_retain + s * g
            ds[lo : lo + 8, :] = ds[lo : lo + 8, :] + g
        filt[16:17, one] = total(t_tail)
        filt[17:18, one] = total(t_retain)
        filt[18:24, one] = jnp.zeros((6, LANES), F32)
        filt[0:17, two] = sums[0:17, one]
        filt[17:18, two] = sums[17:18, one] + sums[18:19, one] * c2
        filt[18:24, two] = jnp.zeros((6, LANES), F32)
        short_back(2, three)
        return unused

    tile_loop(arrive, leave, tile)


def seq_shift(block, along_z, distance):
    pairs = []
    for x in range(4):
        for z in range(4):
            if along_z:
                target = x * 4 + (z + distance) % 4
            else:
                target = (x + distance) % 4 * 4 + z
            pairs.append((x * 4 + z, target))
    return lax.ppermute(block, SEQ, pairs)


def swap(block, axis, bits):
    count = 16 if axis == SEQ else 8
    return lax.ppermute(block, axis, [(i, i ^ bits) for i in range(count)])


def part_shift(block, distance):
    pairs = [(2 * y + c, (y + distance) % 4 * 2 + c) for y in range(4) for c in range(2)]
    return lax.ppermute(block, DP, pairs)


def from_left(block):
    return lax.ppermute(block, SEQ, [(i, i + 1) for i in range(15)])


def from_right(block):
    return lax.ppermute(block, SEQ, [(i + 1, i) for i in range(15)])


def layer_norm(stream, gain, bias):
    average = jnp.mean(stream, axis=-1, keepdims=True)
    centered = stream - average
    variance = jnp.mean(centered * centered, axis=-1, keepdims=True)
    return centered * lax.rsqrt(variance + 1e-05) * gain + bias


def layer_norm_back(stream, gain, grad):
    average = jnp.mean(stream, axis=-1, keepdims=True)
    centered = stream - average
    variance = jnp.mean(centered * centered, axis=-1, keepdims=True)
    scale = lax.rsqrt(variance + 1e-05)
    hat = centered * scale
    grad_gain = jnp.sum(grad * hat, axis=0)
    grad_bias = jnp.sum(grad, axis=0)
    g = grad * gain
    out = scale * (
        g
        - jnp.mean(g, axis=-1, keepdims=True)
        - hat * jnp.mean(g * hat, axis=-1, keepdims=True)
    )
    return out, grad_gain, grad_bias


def positions(place_count, feature_count):
    band_count = (feature_count - 1) // 2
    places = np.arange(place_count, dtype=np.float32)[:, None]
    angles = np.arange(1, band_count + 1, dtype=np.float32)[None, :] * np.float32(
        math.pi / (band_count + 1)
    )
    return np.concatenate(
        [places / np.float32(place_count), np.cos(places * angles), np.sin(places * angles)], axis=1
    )


def dot(a, b):
    return jnp.dot(a, b, preferred_element_type=F32)


def dot_t(a, b):
    return lax.dot_general(a, b, (((1,), (1,)), ((), ())), preferred_element_type=F32)


def dot_w(a, b):
    return lax.dot_general(a, b, (((0,), (0,)), ((), ())), preferred_element_type=F32)


def prepare_kernel(*refs):
    (features, losses, offsets, w1, b1, w2, window, rate, short_weight, short_bias, *vectors) = refs[:18]
    (fp, sw, table, rates, slope, turned, offs, *outs) = refs[18:]
    w1_rows = [w1[j].astype(F32) for j in range(33)]
    short_rows = [short_weight[k].astype(F32) for k in range(3)]
    for layer in range(LAYERS):
        one = slice(layer, layer + 1)
        before = jnp.zeros((24, 64), F32) + b1[one, :].astype(F32)
        for j in range(33):
            before = before + features[:, j : j + 1] * w1_rows[j][one]
        hidden = jnp.sin(before)
        slope[layer] = jnp.cos(before)
        raw = jnp.dot(
            hidden, w2[layer].astype(F32), precision=highest, preferred_element_type=F32
        )
        distance = lax.broadcasted_iota(jnp.int32, (24, 2 * D), 0).astype(F32)
        r = rate[one, :]
        wide_window = window[one, :]
        shaped = raw * jnp.exp(-wide_window * distance)
        loss = losses[one, :]
        table[layer] = shaped
        fp[layer] = shaped
        fp[layer, 16:17, :] = shaped[16:17] * loss
        fp[layer, 17:18, :] = r
        fp[layer, 18:24, :] = jnp.zeros((6, 2 * D), F32)
        rates[layer, 0:1, :] = wide_window
        rates[layer, 1:2, :] = r
        rates[layer, 2:3, :] = loss
        rates[layer, 3:8, :] = jnp.zeros((5, 2 * D), F32)
        square = jnp.concatenate([hidden, jnp.zeros((104, 64), F32)], axis=0)
        square = jnp.concatenate([square, jnp.zeros((128, 64), F32)], axis=1)
        turned[layer] = square.T[0:64]
        for k in range(3):
            sw[layer, k : k + 1, :] = short_rows[k][one]
        sw[layer, 3:4, :] = short_bias[one, :].astype(F32)
        sw[layer, 4:8, :] = jnp.zeros((4, 3 * D), F32)
        for i, vector in enumerate(vectors):
            outs[layer * 9 + i][...] = vector[one, :].astype(F32)
        outs[layer * 9 + 8][0:1, :] = r[:, 0:D]
        outs[layer * 9 + 8][1:2, :] = r[:, D : 2 * D]
        outs[layer * 9 + 8][2:8, :] = jnp.zeros((6, D), F32)
    own = offsets[...]
    offs[64:192, :] = jnp.broadcast_to(own, (128, LANES)).T
    start = offs[64:65, :]
    back = lax.broadcasted_iota(jnp.int32, (64, LANES), 0) - 64
    offs[0:64, :] = jnp.maximum(start + back, 0)
    offs[192:208, :] = jnp.zeros((16, LANES), jnp.int32)


def features_table():
    table = np.zeros((24, LANES), np.float32)
    table[: TAPS + 1, :33] = positions(TAPS + 1, 33)
    return table


class Prepared(typing.NamedTuple):
    fp: typing.Any
    sw: typing.Any
    table: typing.Any
    rates: typing.Any
    slope: typing.Any
    turned: typing.Any
    offs: typing.Any


def prepare(offsets, w):
    vectors = (
        w.ln1_gain,
        w.ln1_bias,
        w.in_bias,
        w.out_bias,
        w.ln2_gain,
        w.ln2_bias,
        w.fc1_bias,
        w.fc2_bias,
    )
    ins = (
        jnp.asarray(features_table()),
        jnp.sqrt(-jnp.expm1(-2.0 * w.decay_rate)),
        offsets,
        w.filter_w1.transpose(1, 0, 2),
        w.filter_b1,
        w.filter_w2,
        w.filter_window,
        w.decay_rate,
        w.short_weight.transpose(1, 0, 2),
        w.short_bias,
    ) + vectors
    outs = [
        ((LAYERS, 24, 2 * D), F32, FAR),
        ((LAYERS, 8, 3 * D), F32, FAR),
        ((LAYERS, 24, 2 * D), F32, FAR),
        ((LAYERS, 8, 2 * D), F32, FAR),
        ((LAYERS, 24, 64), F32, FAR),
        ((LAYERS, 64, LANES), F32, FAR),
        ((208, LANES), jnp.int32, FAR),
    ]
    sizes = [(1, vector.shape[1]) for vector in vectors] + [(8, D)]
    outs += [(size, F32) for _ in range(LAYERS) for size in sizes]
    made = run(prepare_kernel, [(NEAR if i == 1 else FAR, x) for i, x in enumerate(ins)], outs)
    return Prepared(*made[:7]), [Vectors(*made[7 + 9 * i : 16 + 9 * i]) for i in range(LAYERS)]


class Vectors(typing.NamedTuple):
    ln1_gain: typing.Any
    ln1_bias: typing.Any
    in_bias: typing.Any
    out_bias: typing.Any
    ln2_gain: typing.Any
    ln2_bias: typing.Any
    fc1_bias: typing.Any
    fc2_bias: typing.Any
    rates: typing.Any


class Params(typing.NamedTuple):
    ln1_gain: typing.Any
    ln1_bias: typing.Any
    in_weight: typing.Any
    in_bias: typing.Any
    short_weight: typing.Any
    short_bias: typing.Any
    filter_w1: typing.Any
    filter_b1: typing.Any
    filter_w2: typing.Any
    filter_window: typing.Any
    decay_rate: typing.Any
    out_weight: typing.Any
    out_bias: typing.Any
    ln2_gain: typing.Any
    ln2_bias: typing.Any
    fc1_weight: typing.Any
    fc1_bias: typing.Any
    fc2_weight: typing.Any
    fc2_bias: typing.Any


class Saved(typing.NamedTuple):
    stream: typing.Any
    normed: typing.Any
    proj: typing.Any
    gate1: typing.Any
    gate2: typing.Any
    vals: typing.Any
    yloc: typing.Any
    sloc: typing.Any
    pieces: typing.Any
    through: typing.Any
    inner: typing.Any
    outer: typing.Any
    conv2: typing.Any
    state2: typing.Any
    carry: typing.Any
    middle: typing.Any
    normed2: typing.Any
    act: typing.Any
    hidden: typing.Any


def wide(value):
    return value.astype(F32)


def rows_of(layer):
    return slice(192 - LENGTHS[layer], 208)


def forward_layer(layer, stream, where, p, made, v):
    length = LENGTHS[layer]
    normed = layer_norm(stream, v.ln1_gain, v.ln1_bias).astype(BF16)
    proj = (dot(normed, p.in_weight) + v.in_bias).astype(BF16)
    pad = (length + 16, LANES)
    offs = (FAR, made.offs, rows_of(layer))
    fp = (FAR, made.fp, layer)
    gate1, gate2, vals, yloc, sloc, summ = run(
        functools.partial(front_kernel, length),
        [(NEAR, proj), offs, (FAR, made.sw, layer), fp],
        [
            ((length, D), F32, FAR),
            ((length, D), F32, FAR),
            ((length, D), BF16, FAR),
            ((length, D), F32, FAR),
            ((length, D), F32, FAR),
            ((8, D), F32),
        ],
        [(pad, F32), (pad, F32), (pad, F32)],
        tiled=True,
    )
    near = [seq_shift(summ, True, i) for i in (1, 2, 3)]
    total, before, pieces = run(
        join_kernel,
        [(SCALARS, where), (NEAR, summ)] + [(NEAR, x) for x in near] + [(NEAR, v.rates)],
        [((8, D), F32)] * 3,
    )
    far = [seq_shift(total, False, i) for i in (1, 2, 3)]
    inner, outer, conv2, state2, carry, through = run(
        functools.partial(rest_kernel, length),
        [(SCALARS, where), (NEAR, before)]
        + [(NEAR, x) for x in far]
        + [(FAR, gate1), (FAR, gate2), (FAR, yloc), offs, fp],
        [
            ((length, D), BF16, FAR),
            ((length - 32, D), BF16),
            ((length - 32, D), F32, FAR),
            ((length - 32, D), F32, FAR),
            ((8, D), F32, FAR),
            ((8, D), F32, FAR),
        ],
        [((length, LANES), F32), (pad, F32)],
        tiled=True,
    )
    middle = stream[32:] + dot(outer, p.out_weight) + v.out_bias
    normed2 = layer_norm(middle, v.ln2_gain, v.ln2_bias).astype(BF16)
    act = dot(normed2, p.fc1_weight) + v.fc1_bias
    hidden = jax.nn.gelu(act).astype(BF16)
    result = middle + dot(hidden, p.fc2_weight) + v.fc2_bias
    saved = Saved(
        stream=stream,
        normed=normed,
        proj=proj,
        gate1=gate1,
        gate2=gate2,
        vals=vals,
        yloc=yloc,
        sloc=sloc,
        pieces=pieces,
        through=through,
        inner=inner,
        outer=outer,
        conv2=conv2,
        state2=state2,
        carry=carry,
        middle=middle,
        normed2=normed2,
        act=act,
        hidden=hidden,
    )
    return result, saved


def weights_kernel(jobs, split, aliased, small, *refs):
    refs = list(refs)
    where = refs.pop(0)
    pairs = [(refs.pop(0), refs.pop(0)) for _ in jobs]
    extra = refs.pop(0) if small is not None else None
    outs_count = 2 if split else 1
    if aliased:
        refs = refs[outs_count:]
    outs = refs[:outs_count]
    wide_buf, tall_buf, sems, small_sems = refs[outs_count:]
    me = where[2]

    def place(core, parts, side, chunk, row, rows):
        if split and len(outs[core].shape) == 4:
            return outs[core].at[chunk, parts, pl.ds(row, rows)]
        if split:
            return outs[core].at[side, chunk, parts, pl.ds(row, rows)]
        return outs[0].at[parts, core, side, chunk, pl.ds(row, rows)]

    def mine(core):
        return me ^ core if split else core

    every = pl.ds(0, 4)
    waiting = {}
    started = []
    if small is not None:
        for core in range(2):
            copy = pltpu.make_async_copy(
                extra.at[:, mine(core)], place(core, every, 0, 3, small, 64), small_sems.at[core]
            )
            copy.start()
            started.append(copy)
    step = 0
    for (a, g), blocks in zip(pairs, jobs):
        tall = a.shape[1] > D
        turned = None
        for index, copies_of in enumerate(blocks):
            if tall or turned is None:
                left = index * D if tall else 0
                turned = a[:, left : left + D].T
            right = 0 if tall else index * D
            slot = step % 2
            for copy in waiting.pop(slot, ()):
                copy.wait()
            w = jnp.dot(turned, g[:, right : right + D], preferred_element_type=F32).astype(BF16)
            copies = []
            if tall:
                tall_buf[slot] = w.reshape(2, 4, 96, D)
            else:
                wide_buf[slot] = w.reshape(4, 2, 96, D)
            for first, rows, side, chunk, row in copies_of:
                for core in range(2):
                    if tall:
                        source = tall_buf.at[slot, mine(core)]
                        target = place(core, index, side, every, row, 96)
                    else:
                        source = wide_buf.at[slot, :, mine(core), pl.ds(first, rows)]
                        target = place(core, every, side, chunk, row, rows)
                    sem = sems.at[slot, len(copies)]
                    copies.append(pltpu.make_async_copy(source, target, sem))
            for copy in copies:
                copy.start()
            waiting[slot] = copies
            step += 1
    for copies in waiting.values():
        started.extend(copies)
    for copy in started:
        copy.wait()


def weight_grads(where, pairs, jobs, rows, split, small=None, extra=None, onto=None):
    shape = (2, 4, 4, rows, D) if split else (4, 2, 2, 4, rows, D)
    if len(pairs) == 1:
        shape = (4, 4, rows, D)
    outs = [pltpu.HBM(shape, BF16)] * (2 if split else 1)
    operands = [where] + [x for pair in pairs for x in pair]
    in_specs = [smem()] + [vmem()] * (2 * len(pairs))
    if extra is not None:
        operands.append(extra)
        in_specs.append(vmem())
    aliases = {}
    if onto is not None:
        aliases = {len(operands) + i: i for i in range(len(outs))}
        operands += [in_hbm(x) for x in onto]
        in_specs += [pl.BlockSpec(memory_space=pltpu.HBM)] * len(outs)
    tokens = pairs[0][0].shape[0]
    blocks = sum(len(job) for job in jobs)
    return pl.pallas_call(
        functools.partial(weights_kernel, jobs, split, onto is not None, small),
        out_shape=outs,
        in_specs=in_specs,
        out_specs=[pl.BlockSpec(memory_space=pltpu.HBM)] * len(outs),
        input_output_aliases=aliases,
        scratch_shapes=[
            pltpu.VMEM((2, 4, 2, 96, D), BF16),
            pltpu.VMEM((2, 2, 4, 96, D), BF16),
            pltpu.SemaphoreType.DMA((2, 4)),
            pltpu.SemaphoreType.DMA((2,)),
        ],
        compiler_params=pltpu.CompilerParams(vmem_limit_bytes=VMEM_LIMIT),
        cost_estimate=pl.CostEstimate(
            flops=2 * 256 * D * D * blocks, bytes_accessed=2 * D * D * blocks, transcendentals=0
        ),
    )(*operands)


def ff_jobs(row):
    fc1 = tuple(((0, 96, 0, chunk, row),) for chunk in range(4))
    fc2 = tuple(((0, 96, 1, None, row),) for _ in range(4))
    return fc1, fc2


def mix_jobs(row):
    def low(side):
        return ((0, 64, side, 0, row), (64, 32, side, 1, row))

    def high(side):
        return ((0, 32, side, 1, row + 32), (32, 64, side, 2, row))

    return (low(1), high(1), low(0)), (high(0),)


def small_kernel(*refs):
    vectors = refs[:6]
    fc1_bias, columns, filt, table, rates, w2, turned, slope, out, buf, draw, narrow = refs[6:]
    window, rate, loss = rates[0:1, :], rates[1:2, :], rates[2:3, :]
    far = filt[TAPS : TAPS + 1, :]
    dwindow = jnp.zeros((1, 2 * D), F32)
    for k in range(TAPS + 1):
        d = filt[k : k + 1, :] * (loss if k == TAPS else 1.0)
        dwindow = dwindow - float(k) * table[k : k + 1, :] * d
        draw[k : k + 1, :] = d * jnp.exp(-window * float(k))
    draw[17:18, :] = dwindow
    draw[18:19, :] = (
        far * table[TAPS : TAPS + 1, :] * jnp.exp(-2.0 * rate) / loss
        - filt[TAPS + 1 : TAPS + 2, :] * jnp.exp(-rate)
    )
    draw[19:24, :] = jnp.zeros((5, 2 * D), F32)
    dhidden = lax.dot_general(
        draw[...],
        w2[...].astype(F32),
        (((1,), (1,)), ((), ())),
        precision=highest,
        preferred_element_type=F32,
    )
    dbefore = dhidden * slope[...]
    dw1 = jnp.zeros((40, 64), F32)
    for k in range(TAPS + 1):
        dw1 = dw1 + turned[:, k : k + 1] * dbefore[k : k + 1, :]
    narrow[...] = dw1
    buf[...] = jnp.zeros((64, D), F32)

    def columns_of(value, part, width):
        return pltpu.roll(value, (value.shape[1] - part * width) % value.shape[1], 1)[:, :width]

    pad64 = jnp.zeros((40, 64), F32)
    tall = jnp.concatenate([narrow[...], pad64], axis=1)
    flat = jnp.concatenate([v[...] for v in vectors] + [jnp.zeros((2, D), F32)], axis=0)
    for part in range(8):
        buf[0:6, 0:96] = columns_of(flat, part, 96)[0:6]
        buf[6:7, 0:384] = fc1_bias[:, part * 384 : (part + 1) * 384]
        buf[7:12, 0:288] = columns_of(columns[...], part, 288)[0:5]
        buf[12:31, 0:192] = columns_of(draw[...], part, 192)[0:19]
        mine = columns_of(tall, part, 8)
        buf[31:64, 0:8] = mine[0:33]
        buf[6:7, 384:392] = mine[33:34]
        out[part // 2, part % 2] = buf[...].astype(BF16)


def turned_features():
    table = np.zeros((40, LANES), np.float32)
    table[:33, : TAPS + 1] = positions(TAPS + 1, 33).T
    table[33, : TAPS + 1] = 1.0
    return table


def backward_layer(layer, grad, where, p, made, v, s, beside=None):
    length = LENGTHS[layer]
    first = layer == 0
    offs = (FAR, made.offs, rows_of(layer))
    fp = (FAR, made.fp, layer)
    grad_fc2_bias = jnp.sum(grad, axis=0)
    grad_low = grad.astype(BF16)
    dhidden = dot_t(grad_low, p.fc2_weight)
    dact = jax.vjp(jax.nn.gelu, s.act)[1](dhidden)[0]
    grad_fc1_bias = jnp.sum(dact, axis=0)
    dact_low = dact.astype(BF16)
    dnormed2 = dot_t(dact_low, p.fc1_weight)
    dmiddle, grad_ln2_gain, grad_ln2_bias = layer_norm_back(s.middle, v.ln2_gain, dnormed2)
    dmiddle = dmiddle + grad
    grad_out_bias = jnp.sum(dmiddle, axis=0)
    dmiddle_low = dmiddle.astype(BF16)
    dout = dot_t(dmiddle_low, p.out_weight)
    pad = (length + 16, LANES)
    dinner, sums, direct = run(
        functools.partial(back_kernel, length),
        [
            (NEAR, dout),
            (FAR, s.gate1),
            (FAR, s.gate2),
            (FAR, s.state2),
            (FAR, s.inner),
            offs,
            fp,
        ],
        [((length, D), F32, FAR), ((24, D), F32, FAR), ((8, D), F32)],
        [(pad, F32), (pad, F32), (pad, F32), ((length, LANES), F32)],
        tiled=True,
    )
    near = [seq_shift(direct, True, i) for i in (1, 2, 3)]
    ff = weight_grads(
        where, [(s.normed2, dact_low), (s.hidden, grad_low)], ff_jobs(0), 96, False
    )[0]
    near, ff = lax.optimization_barrier((near, ff))
    ff = lax.psum_scatter(ff.reshape(8, 2, 4, 96, D), DP, scatter_dimension=0, tiled=False)
    total, after = run(
        join_back_kernel,
        [(SCALARS, where), (NEAR, direct)]
        + [(NEAR, x) for x in near]
        + [(NEAR, s.pieces), (NEAR, v.rates)],
        [((8, D), F32)] * 2,
    )
    far = [seq_shift(total, False, i) for i in (1, 2, 3)]
    if first:
        beside = [add(beside[0][side], beside[1][side]) for side in range(2)]
    far, beside = lax.optimization_barrier((far, beside))
    dproj, colsums, filt = run(
        functools.partial(end_kernel, length),
        [(SCALARS, where), (NEAR, after)]
        + [(NEAR, x) for x in far]
        + [
            (FAR, s.through),
            (FAR, dinner),
            (NEAR, dout),
            (FAR, s.conv2),
            (FAR, s.gate1),
            (FAR, s.yloc),
            (FAR, s.sloc),
            (FAR, s.vals),
            (FAR, s.carry),
            (FAR, s.proj),
            offs,
            (FAR, made.sw, layer),
            fp,
            (FAR, sums),
        ],
        [((length, 3 * D), BF16), ((8, 3 * D), F32), ((24, 2 * D), F32)],
        [(pad, F32)] * 5,
        tiled=True,
    )
    pairs = [(s.normed, dproj), (s.outer, dmiddle_low)]
    if first:
        mix = weight_grads(where, pairs, mix_jobs(0), 64, True)
        dproj, mix = lax.optimization_barrier((dproj, mix))
        mix_came = swap(mix[1], DP, 1)
    dnormed = dot_t(dproj, p.in_weight)
    dstream, grad_ln1_gain, grad_ln1_bias = layer_norm_back(s.stream, v.ln1_gain, dnormed)
    dstream = dstream + jnp.concatenate([jnp.zeros((32, D), F32), dmiddle], axis=0)
    vectors = (
        grad_ln1_gain,
        grad_ln1_bias,
        grad_out_bias,
        grad_ln2_gain,
        grad_ln2_bias,
        grad_fc2_bias,
        grad_fc1_bias,
    )
    small = run(
        small_kernel,
        [(NEAR, vector.reshape(1, -1)) for vector in vectors]
        + [
            (NEAR, colsums),
            (NEAR, filt),
            (FAR, made.table, layer),
            (FAR, made.rates, layer),
            (FAR, p.filter_w2, layer),
            (FAR, jnp.asarray(turned_features())),
            (FAR, made.slope, layer),
        ],
        [((4, 2, 64, D), BF16)],
        [((64, D), F32), ((24, 2 * D), F32), ((40, 64), F32)],
    )[0]
    if first:
        own = take(small, where[2], 1, 1)
        other = swap(take(small, 1 - where[2], 1, 1), DP, 1)
        mix = [
            jnp.concatenate([add(mix[0][side], mix_came[side]), beside[side]], axis=2)
            for side in range(2)
        ]
        mix[0] = lax.dynamic_update_slice(mix[0], add(own, other)[None], (3, 0, 0, 0))
    else:
        mix = weight_grads(where, pairs, mix_jobs(0), 64, True, 0, small)
        mix = (mix[0], swap(mix[1], DP, 1))
    return dstream, ff, mix, beside


def add(*values):
    total = wide(values[0])
    for value in values[1:]:
        total = total + wide(value)
    return total.astype(BF16)


class Ring(typing.NamedTuple):
    me: typing.Any
    shift: typing.Any


def take(block, index, axis=0, bits=3):
    return lax.dynamic_index_in_dim(block, index & bits, axis, keepdims=False)


def scatter_direct(ring, block, axis):
    parts = [take(block, ring.me, axis)]
    parts += [ring.shift(take(block, ring.me + i, axis), i) for i in (1, 2, 3)]
    return add(*parts)


def both_ways(ring, pair):
    return ring.shift(pair[0], 1), ring.shift(pair[1], 3)


def scatter_ring(ring, block, dim):
    far = take(block, ring.me + 2)
    half = far.shape[dim] // 2
    up, down = both_ways(
        ring,
        (
            lax.slice_in_dim(far, 0, half, axis=dim),
            lax.slice_in_dim(far, half, 2 * half, axis=dim),
        ),
    )
    none = jnp.zeros_like(up)
    up = jnp.concatenate([up, none], axis=dim)
    down = jnp.concatenate([none, down], axis=dim)
    came = both_ways(
        ring, (add(take(block, ring.me + 1), up), add(take(block, ring.me - 1), down))
    )
    return add(take(block, ring.me), *came)


def gather_direct(ring, block):
    return jnp.stack([block] + [ring.shift(block, i) for i in (1, 2, 3)])


def gather_ring(ring, block):
    half = block.shape[0] // 2
    before = ring.shift(block, 1)
    after = ring.shift(block, 3)
    return block, before, after, ring.shift(before[:half], 1), ring.shift(after[half:], 3)


def unpack_kernel(where, turned, *refs):
    sides = (refs[0:5], refs[5:10])
    inw, outw, fc1, fc2 = refs[10:14]
    small = refs[14:29]
    rows, mixed = refs[29:]
    for side, (own, before, after, far_low, far_high) in enumerate(sides):
        ring = where[side]
        other = where[1 - side]
        for distance, pieces in (
            (0, ((own, 0, 4),)),
            (1, ((before, 0, 4),)),
            (3, ((after, 0, 4),)),
            (2, ((far_low, 0, 2), (far_high, 2, 4))),
        ):
            chunk = (ring - distance) & 3
            for ref, low, high in pieces:
                for i in range(low, high):
                    at = pl.multiple_of(((other - i) & 3) * 40, 8)
                    for layer in range(LAYERS):
                        rows[layer, pl.ds(at, 40), :] = ref[i - low, layer].astype(F32)
            for layer in range(LAYERS):
                if side == 0:
                    fc1[layer, :, pl.ds(pl.multiple_of(chunk * D, D), D)] = rows[layer, 0:96, :]
                else:
                    fc2[layer, pl.ds(pl.multiple_of(chunk * 96, 96), 96), :] = rows[layer, 0:96, :]
                mixed[side, layer, pl.ds(pl.multiple_of(chunk * 64, 64), 64), :] = rows[
                    layer, 96:160, :
                ]
    (
        ln1_gain,
        ln1_bias,
        out_bias,
        ln2_gain,
        ln2_bias,
        fc2_bias,
        fc1_bias,
        in_bias,
        short_weight,
        short_bias,
        filter_w1,
        filter_b1,
        filter_w2,
        window,
        decay,
    ) = small
    for layer in range(LAYERS):
        inw[layer, :, 0:D] = mixed[1, layer, 0:96, :]
        inw[layer, :, D : 2 * D] = mixed[1, layer, 96:192, :]
        inw[layer, :, 2 * D : 3 * D] = mixed[0, layer, 0:96, :]
        outw[layer] = mixed[0, layer, 96:192, :]
        one = pl.ds(layer, 1)
        for row, out in enumerate((ln1_gain, ln1_bias, out_bias, ln2_gain, ln2_bias, fc2_bias)):
            out[one, :] = mixed[0, layer, 192 + row : 193 + row, 0:96]
        fc1_bias[one, :] = mixed[0, layer, 198:199, 0:384]
        filter_b1[one, :] = mixed[0, layer, 198:199, 384:392]
        in_bias[one, :] = mixed[0, layer, 199:200, 0:288]
        for k in range(3):
            short_weight[k, one, :] = mixed[0, layer, 200 + k : 201 + k, 0:288]
        short_bias[one, :] = mixed[0, layer, 203:204, 0:288]
        window[one, :] = mixed[0, layer, 221:222, 0:192]
        decay[one, :] = mixed[0, layer, 222:223, 0:192]
        filter_w1[layer] = mixed[0, layer, 223:256, 0:8]
        total = jnp.zeros((64, 192), F32)
        for k in range(TAPS + 1):
            draw = mixed[0, layer, 204 + k : 205 + k, 0:192]
            total = total + turned[layer, :, k : k + 1] * draw
        filter_w2[layer] = total


def side_rings(where):
    return (
        Ring(where[0], lambda block, i: seq_shift(block, False, i)),
        Ring(where[1], lambda block, i: seq_shift(block, True, i)),
    )


def reduce_grads(where, turned, ff, mix):
    rings = side_rings(where)
    y_ring = Ring(where[3], part_shift)
    sides = [scatter_ring(ring, mix[side], 1) for side, ring in enumerate(rings)]
    sides, ff = lax.optimization_barrier((sides, ff))
    mix = scatter_ring(y_ring, jnp.stack(sides, axis=1), 0).reshape(2, LAYERS, 64, D)
    sums = []
    for side, ring in enumerate(rings):
        block = jnp.concatenate([ff[0][side], ff[1][side]], axis=1)
        sums.append(scatter_direct(ring, block, 0).reshape(LAYERS, 96, D))
    pieces = []
    for side in range(2):
        other = rings[1 - side]
        two = jnp.concatenate([sums[side], mix[side]], axis=1).reshape(2, 4, 40, D)
        own = scatter_direct(other, two, 1)
        pieces.extend(gather_ring(rings[side], gather_direct(other, own)))
    shapes = [(LAYERS, 96, 3 * D), (LAYERS, 96, D), (LAYERS, 96, FF), (LAYERS, 384, D)]
    shapes += [(LAYERS, 96)] * 6 + [(LAYERS, 384), (LAYERS, 288), (3, LAYERS, 288), (LAYERS, 288)]
    shapes += [(LAYERS, 33, 8), (LAYERS, 8), (LAYERS, 64, 192)] + [(LAYERS, 192)] * 2
    return pl.pallas_call(
        unpack_kernel,
        out_shape=[jax.ShapeDtypeStruct(shape, F32) for shape in shapes],
        in_specs=[smem()] + [vmem()] * 11,
        out_specs=[vmem()] * len(shapes),
        scratch_shapes=[
            pltpu.VMEM((LAYERS, 160, D), F32),
            pltpu.VMEM((2, LAYERS, 256, D), F32),
        ],
        compiler_params=pltpu.CompilerParams(vmem_limit_bytes=24 * 1024 * 1024),
    )(where, turned, *pieces)


def body(tokens, out_grad, offsets, *weights):
    part = lax.axis_index(DP).astype(jnp.int32)
    place = lax.axis_index(SEQ).astype(jnp.int32)
    where = jnp.stack([place // 4, place % 4, part % 2, part // 2])
    weights = Params(*weights)
    made, vectors = prepare(offsets, weights)
    params = [
        weights._replace(
            in_weight=weights.in_weight[layer],
            out_weight=weights.out_weight[layer],
            fc1_weight=weights.fc1_weight[layer],
            fc2_weight=weights.fc2_weight[layer],
        )
        for layer in range(LAYERS)
    ]
    own = tokens[0]
    halo = from_left(own[BLK - 64 :])
    stream = jnp.concatenate([halo, own], axis=0).astype(F32)
    saved = []
    for layer in range(LAYERS):
        stream, kept = forward_layer(layer, stream, where, params[layer], made, vectors[layer])
        saved.append(kept)
    mixed = stream.astype(BF16)[None]
    grad = out_grad[0].astype(F32)
    grad, ff_last, mix_last, mixed = backward_layer(
        1, grad, where, params[1], made, vectors[1], saved[1], mixed
    )
    grad, kept = lax.optimization_barrier((grad, mix_last[0]))
    grad, ff_first, mix_first, _ = backward_layer(
        0, grad, where, params[0], made, vectors[0], saved[0], (kept, mix_last[1])
    )
    returned = from_right(grad[:64])
    input_grad = jnp.concatenate([grad[64:128], grad[128:] + returned], axis=0)[None]
    found = reduce_grads(where, made.turned, (ff_first, ff_last), mix_first)
    grads = Params(
        in_weight=found[0],
        out_weight=found[1],
        fc1_weight=found[2],
        fc2_weight=found[3],
        ln1_gain=found[4],
        ln1_bias=found[5],
        out_bias=found[6],
        ln2_gain=found[7],
        ln2_bias=found[8],
        fc2_bias=found[9],
        fc1_bias=found[10],
        in_bias=found[11],
        short_weight=found[12].transpose(1, 0, 2),
        short_bias=found[13],
        filter_w1=found[14],
        filter_b1=found[15],
        filter_w2=found[16],
        filter_window=found[17],
        decay_rate=found[18],
    )
    return (mixed, input_grad) + tuple(grads)


def solution(mesh):
    block = P(DP, SEQ, None)
    rows = P(None, DP, None)
    columns = P(None, None, DP)
    vector = P(None, DP)
    outs = Params(*([vector] * len(Params._fields)))._replace(
        in_weight=rows,
        out_weight=rows,
        fc1_weight=rows,
        fc2_weight=rows,
        short_weight=columns,
        filter_w1=columns,
        filter_w2=columns,
    )
    return jax.shard_map(
        body,
        mesh=mesh,
        in_specs=(block, block, P(DP, SEQ)) + (P(),) * len(outs),
        out_specs=(block, block) + tuple(outs),
        check_vma=False,
    )
```
